32 devices in a mesh: row: 16 (over z, y, core), col: 2 (over x).
Axes of the slice: x: 2, y: 2, z: 4, core: 2. Of those that a mesh axis runs over, the one named last changes fastest.
Arguments:
- p_vals: float32 [64, 4, 128, 128], P('row', 'col'), may hold values from -2 to 2
- p_cols: int32 [64, 4], P('row'), may hold values from 0 to 63, as said below
- out_cols: int32 [64, 4], P('row'), may hold values from 0 to 63, as said below
Outputs:
- c_vals: float32 [64, 4, 128, 128], P('row', 'col')
The draws below stay inside these ranges and needn't reach their ends.
Inputs may be any that keep to these rules, and one draw needn't show every extreme that they name: Block column indices; p_cols[i, s] // 4 equals (i // 4 + s // 2 - t) mod 16 for some t of 0, 1, 2, 3. `out_cols`: each output block column is p_cols[p_cols[i, s], s2] for some slots s and s2.
All inputs are finite; a program needn't handle non-finite values.
Results may differ from the reference program's by a relative error of at most 0.0003.
Values sent between devices are 32-bit elements; how exact they have to be, the bound alone decides.
No kernel may reach another device: no remote copies, remote signals or barrier semaphores. Data moves between devices by JAX's collectives and lax.ppermute only.
A program may use at most 64 MiB of HBM per device.

```python
import jax
import jax.numpy as jnp
from jax import lax

BS = 128
BR = 4
S_DEV = 2
NB = 64
S = 4
SO = 4
N_ROW = 16


def pattern_both(key):
    key_pat = jax.random.fold_in(key, 11)
    k_off, k_loc, k_s, k_t = jax.random.split(key_pat, 4)
    group = jnp.arange(NB, dtype=jnp.int32) // BR
    slot_dev = jnp.arange(S, dtype=jnp.int32) // S_DEV
    step_off = jax.random.randint(k_off, (NB, S), 0, 4, dtype=jnp.int32)
    local_row = jax.random.randint(k_loc, (NB, S), 0, BR, dtype=jnp.int32)
    target = (group[:, None] + slot_dev[None, :] - step_off) % N_ROW
    cols = target * BR + local_row
    first = jax.random.randint(k_s, (NB, SO), 0, S, dtype=jnp.int32)
    second = jax.random.randint(k_t, (NB, SO), 0, S, dtype=jnp.int32)
    middle = jnp.take_along_axis(cols, first, axis=1)
    outs = cols[middle, second]
    return (cols, outs)


def draw_p_cols(key, part):
    return pattern_both(key)[0]


def draw_out_cols(key, part):
    return pattern_both(key)[1]


def levels(stream_key, dims, pieces, smallest, largest):
    level, own = 1.0, jax.random.fold_in(stream_key, 6)
    for position, parts in pieces:
        draws = jnp.exp(jax.random.uniform(jax.random.fold_in(own, position), (parts,), jnp.float32, smallest / len(pieces), largest / len(pieces)))
        level = level * jnp.repeat(draws, dims[position] // parts).reshape([-1 if axis == position else 1 for axis in range(len(dims))])
    return level


def normal_values(own_key, extent, scale, reach, pieces=(), kind=jnp.bfloat16):
    array = scale * jax.random.normal(own_key, extent, jnp.float32)
    if pieces:
        array = array * levels(own_key, extent, pieces, -0.22, 0.18)
    return jnp.clip(array, -reach, reach).astype(kind)


def setup_inputs(seed: int = 0) -> dict:
    key_list = jax.random.split(jax.random.key(seed), 4)
    p_vals = normal_values(key_list[0], (NB, S, BS, BS), 0.3, 2.0, ((0, 16), (1, 2)), jnp.float32)
    p_cols = draw_p_cols(jax.random.fold_in(key_list[3], 71), 0)
    out_cols = draw_out_cols(jax.random.fold_in(key_list[3], 71), 0)
    return {"p_vals": p_vals, "p_cols": p_cols, "out_cols": out_cols}


def reference(p_vals, p_cols, out_cols):
    group = jnp.arange(NB, dtype=jnp.int32) // BR
    slot_dev = jnp.arange(S, dtype=jnp.int32) // S_DEV
    offset = (group[:, None] + slot_dev[None, :] - p_cols // BR) % N_ROW
    window = (offset < 3).astype(jnp.float32)

    def one_row(items):
        vals_row, cols_row, outs_row, weight_row = items
        blocks = p_vals[cols_row]
        inner = p_cols[cols_row]
        match = (inner[:, :, None] == outs_row[None, None, :]).astype(jnp.float32)
        mixed = jnp.einsum("sto,stab->soab", match, blocks, precision=lax.Precision.HIGHEST)
        left = vals_row * weight_row[:, None, None]
        return jnp.einsum("sab,sobc->oac", left, mixed, precision=lax.Precision.HIGHEST)

    return lax.map(one_row, (p_vals, p_cols, out_cols, window))
```

```python
import functools

import jax
import jax.numpy as jnp
from jax import lax
from jax.experimental import pallas as pl
from jax.experimental.pallas import tpu as pltpu
from jax.sharding import PartitionSpec as P

WINDOW = 3
HBM = pl.BlockSpec(memory_space=pltpu.HBM)
SMEM = pl.BlockSpec(memory_space=pltpu.SMEM)


def split(x):
    high = x.astype(jnp.bfloat16)
    return high, (x - high.astype(jnp.float32)).astype(jnp.bfloat16)


def product_kernel(n_left, layers, has_total, *refs):
    refs = list(refs)
    place, weight = refs.pop(0), refs.pop(0)
    left_hbm = [refs.pop(0) for _ in range(n_left)]
    right_hbm = [[refs.pop(0) for _ in range(n)] for n in layers]
    total_hbm = refs.pop(0) if has_total else None
    out_ref = refs.pop(0)
    left = refs.pop(0)
    right = [refs.pop(0) for _ in layers]
    total = refs.pop(0) if has_total else None
    high, low, sems = refs
    rows, slots, block = left.shape[0], left.shape[1], left.shape[3]
    slots_dev = slots // n_left
    outs = out_ref.shape[1]

    copies = []

    def bring(source, target):
        copy = pltpu.make_async_copy(source, target, sems.at[len(copies)])
        copy.start()
        copies.append(copy)

    for at, source in enumerate(left_hbm):
        bring(source, left.at[:, pl.ds(at * slots_dev, slots_dev)])
    for sources, target in zip(right_hbm, right):
        for at, source in enumerate(sources):
            bring(source, target.at[pl.ds(at * rows, rows)])
    if has_total:
        bring(total_hbm, total)
    for copy in copies:
        copy.wait()

    def one_row(i, carry):
        for s in range(slots):
            mixed = [jnp.zeros((block, block), jnp.float32) for _ in range(outs)]
            for layer in range(len(layers)):
                at = (layer * rows + i) * slots + s
                row = place[at]
                for t in range(slots_dev):
                    tile = right[layer][row, t]
                    for o in range(outs):
                        mixed[o] += weight[(at * slots_dev + t) * outs + o] * tile
            for o in range(outs):
                here = (pl.ds(s * block, block), pl.ds(o * block, block))
                high[here], low[here] = split(mixed[o])
        left_high, left_low = split(jnp.concatenate([left[i, s] for s in range(slots)], axis=1))
        dot = functools.partial(jnp.dot, preferred_element_type=jnp.float32)
        result = dot(left_high, high[...]) + (dot(left_high, low[...]) + dot(left_low, high[...]))
        for o in range(outs):
            piece = result[:, o * block:(o + 1) * block]
            out_ref[i, o] = piece + total[i, o] if has_total else piece
        return carry

    lax.fori_loop(0, rows, one_row, 0)


def add_products(place, weight, left, layers, total):
    rows, slots_dev, block = left[0].shape[:3]
    slots = len(left) * slots_dev
    sizes = tuple(len(layer) for layer in layers)
    operands = [*left, *(x for layer in layers for x in layer)] + ([] if total is None else [total])
    shape = jax.ShapeDtypeStruct(left[0].shape, jnp.float32)
    scratch = [pltpu.VMEM((rows, slots, block, block), jnp.float32)]
    scratch += [pltpu.VMEM((n * rows, slots_dev, block, block), jnp.float32) for n in sizes]
    if total is not None:
        scratch.append(pltpu.VMEM(shape.shape, jnp.float32))
    scratch += [pltpu.VMEM((slots * block, slots_dev * block), jnp.bfloat16)] * 2
    scratch.append(pltpu.SemaphoreType.DMA((len(operands),)))
    flops = 2 * rows * slots * slots_dev * block**3 * 3
    return pl.pallas_call(
        functools.partial(product_kernel, len(left), sizes, total is not None),
        out_shape=shape,
        in_specs=[SMEM, SMEM] + [HBM] * len(operands),
        out_specs=pl.BlockSpec(memory_space=pltpu.VMEM),
        scratch_shapes=scratch,
        compiler_params=pltpu.CompilerParams(vmem_limit_bytes=48 * 2**20),
        cost_estimate=pl.CostEstimate(flops=flops, bytes_accessed=4 * left[0].size * (len(operands) + 1), transcendentals=0),
    )(jnp.concatenate([x.reshape(-1) for x in place]), jnp.concatenate([x.reshape(-1) for x in weight]), *operands)


def on_device(p_vals, p_cols, out_cols):
    rows, slots_dev = p_vals.shape[:2]
    slots, outs_dev = p_cols.shape[1], out_cols.shape[1] // lax.axis_size("col")
    nrow, ncol = lax.axis_size("row"), lax.axis_size("col")
    row_at, col_at = lax.axis_index("row"), lax.axis_index("col")

    def permute(x, source):
        pairs = []
        for r in range(nrow):
            for c in range(ncol):
                if source(r, c) is not None:
                    from_row, from_col = source(r, c)
                    pairs.append((from_row % nrow * ncol + from_col % ncol, r * ncol + c))
        return lax.ppermute(x, ("row", "col"), pairs)

    ring = jnp.concatenate([p_cols, p_cols], axis=1)
    cols_here = lax.dynamic_slice_in_dim(ring, col_at * slots_dev, slots, 1)
    halves = (col_at + jnp.arange(slots, dtype=jnp.int32) // slots_dev) % ncol
    group = cols_here // rows
    live = (row_at + halves[None, :] - group) % nrow < WINDOW
    outs_here = lax.dynamic_slice_in_dim(out_cols, col_at * outs_dev, outs_dev, 1)
    cols_at = {d: permute(p_cols, lambda r, c, d=d: (r + d, c)) for d in range(1 - WINDOW, ncol) if d}
    cols_at[0] = p_cols

    def weights(offsets, tables, half):
        found = (group[:, :, None] - row_at - jnp.stack(offsets)) % nrow == 0
        inside = jnp.any(found, axis=2)
        position = jnp.sum(jnp.where(found, jnp.arange(len(offsets), dtype=jnp.int32), 0), axis=2)
        place = jnp.where(inside, position * rows + cols_here % rows, 0)
        table = lax.dynamic_slice_in_dim(jnp.concatenate(tables, axis=0), half * slots_dev, slots_dev, 1)
        chosen = place[:, :, None] == jnp.arange(table.shape[0], dtype=jnp.int32)
        inner = jnp.sum(jnp.where(chosen[:, :, :, None], table[None, None], 0), axis=2)
        match = inner[:, :, :, None] == outs_here[:, None, None, :]
        return place, (match & (live & inside)[:, :, None, None]).astype(jnp.float32)

    if ncol == 2 and nrow % 2 == 0:
        even = row_at % 2 == 0

        def by_core(from_even, from_odd):
            return lambda r, c: (from_odd if r % 2 else from_even)(r, c)

        def across(r, c):
            return r, c + 1

        def behind(r, c):
            return r - 2, c

        def ahead(r, c):
            return r + 2, c

        def beside(r, c):
            return r ^ 1, c

        def none(r, c):
            return None

        first = permute(p_vals, by_core(across, behind))
        second = permute(p_vals, by_core(behind, across))
        beside_own = permute(p_vals, beside)
        third = permute(first, by_core(ahead, across))
        late_own, _ = lax.optimization_barrier((p_vals, first))
        fifth = permute(late_own, by_core(none, lambda r, c: (r + 1, c)))
        fourth = permute(second, by_core(across, none))
        beside_first = permute(first, beside)
        beside_second = permute(second, by_core(beside, none))
        beside_third = permute(third, beside)

        def pick(x, y):
            return jnp.where(even, x, y)

        other = pick(first, second)
        near, far = pick(1, -1), pick(-1, 1)
        near_cols, far_cols = pick(cols_at[1], cols_at[-1]), pick(cols_at[-1], cols_at[1])
        back = jnp.int32(-2)
        zero = jnp.int32(0)
        mate = (col_at + 1) % ncol
        place_c, weight_c = weights([zero, near, back, far], [p_cols, near_cols, cols_at[-2], far_cols], col_at)
        place_n, weight_n = weights([zero, near], [p_cols, near_cols], mate)
        place_l, weight_l = weights([back, far], [cols_at[-2], far_cols], mate)
        left = [p_vals, other]
        total = add_products(
            [place_c, place_n],
            [weight_c, weight_n],
            left,
            [
                [p_vals, beside_own, pick(second, first), pick(beside_first, fifth)],
                [other, pick(beside_second, beside_first)],
            ],
            None,
        )
        return add_products([place_l], [weight_l], left, [[pick(fourth, third), beside_third]], total)

    left = [p_vals] + [permute(p_vals, lambda r, c, j=j: (r, c + j)) for j in range(1, ncol)]
    offsets = list(range(1 - WINDOW, ncol))
    shards = [p_vals if d == 0 else permute(p_vals, lambda r, c, d=d: (r + d, c)) for d in offsets]
    total = None
    for j in range(ncol):
        layer = shards if j == 0 else [permute(x, lambda r, c, j=j: (r, c + j)) for x in shards]
        tables = [cols_at[d] for d in offsets]
        place, weight = weights([jnp.int32(d) for d in offsets], tables, (col_at + j) % ncol)
        total = add_products([place], [weight], left, [layer], total)
    return total


def solution(mesh):
    placed = (P("row", "col", None, None), P("row", None), P("row", None))
    return jax.shard_map(
        on_device,
        mesh=mesh,
        in_specs=placed,
        out_specs=P("row", "col", None, None),
        check_vma=False,
    )
```

```python
import functools

import jax
import jax.numpy as jnp
from jax import lax
from jax.experimental import pallas as pl
from jax.experimental.pallas import tpu as pltpu
from jax.sharding import PartitionSpec as P

WINDOW = 3
SUBLANES = 8
SMEM = pl.BlockSpec(memory_space=pltpu.SMEM)
VMEM = pl.BlockSpec(memory_space=pltpu.VMEM)
PARAMS = pltpu.CompilerParams(vmem_limit_bytes=48 * 2**20)
SOON = pl.CostEstimate(flops=0, bytes_accessed=0, transcendentals=0)


def split(x):
    high = x.astype(jnp.bfloat16)
    return high, (x - high.astype(jnp.float32)).astype(jnp.bfloat16)


def tail_rows(rows):
    return -(-2 * rows // SUBLANES) * SUBLANES


def by_parity(paired, run):
    if paired:
        parity = lax.rem(lax.axis_index("row"), 2)
        pl.when(parity == 0)(lambda: run(0))
        pl.when(parity == 1)(lambda: run(1))
    else:
        run(None)


def parcel(sources, tables):
    tall, block = min(x.shape for x in sources)
    rows, slots = tables[0].shape
    tail = tail_rows(rows)
    paired = len(sources) > 1

    def kernel(*refs):
        cols_refs, refs, (out_ref, sem) = refs[:len(tables)], refs[len(tables):-2], refs[-2:]

        def run(p):
            copy = pltpu.make_async_copy(refs[p or 0].at[pl.ds(0, tall)], out_ref.at[pl.ds(0, tall)], sem)
            copy.start()
            row, column = (lax.broadcasted_iota(jnp.int32, (tail, block), d) for d in (0, 1))
            cols = jnp.zeros((tail, block), jnp.float32)
            for n, ref in enumerate(cols_refs):
                for r in range(rows):
                    for s in range(slots):
                        here = (row == n * rows + r) & (column == s)
                        cols = jnp.where(here, ref[r, s].astype(jnp.float32), cols)
            out_ref[pl.ds(tall, tail)] = cols
            copy.wait()

        by_parity(paired, run)

    return pl.pallas_call(
        kernel,
        out_shape=jax.ShapeDtypeStruct((tall + tail, block), jnp.float32),
        in_specs=[SMEM] * len(tables) + [VMEM] * len(sources),
        out_specs=VMEM,
        scratch_shapes=[pltpu.SemaphoreType.DMA],
        compiler_params=PARAMS,
        cost_estimate=SOON,
    )(*tables, *sources)


def index_tile(source, tall):
    def kernel(source_ref, out_ref, sem):
        copy = pltpu.make_async_copy(source_ref.at[pl.ds(tall, out_ref.shape[0])], out_ref, sem)
        copy.start()
        copy.wait()

    return pl.pallas_call(
        kernel,
        out_shape=jax.ShapeDtypeStruct((source.shape[0] - tall, source.shape[1]), jnp.float32),
        in_specs=[VMEM],
        out_specs=VMEM,
        scratch_shapes=[pltpu.SemaphoreType.DMA],
        compiler_params=PARAMS,
        cost_estimate=pl.CostEstimate(flops=10**9, bytes_accessed=0, transcendentals=0),
    )(source)


def add_products(p_cols, out_cols, left, entries, total, paired):
    rows, slots = p_cols.shape
    ncol = len(left)
    slots_dev = slots // ncol
    outs = out_cols.shape[1] // ncol
    block = left[0][0].shape[1]
    nrow = lax.axis_size("row")
    shards, indices = [], [p_cols, out_cols]

    def number(array, known):
        for n, x in enumerate(known):
            if x is array:
                return n
        known.append(array)
        return len(known) - 1

    left_at = [[number(x, shards) for x in part] for part in left]
    plan, parcels = [], []
    for d, p, (cols, start), pieces, lefts in entries:
        is_parcel = cols.dtype == jnp.float32
        source = number(number(cols, shards), parcels) if is_parcel else number(cols, indices)
        plan.append((d, p, is_parcel, source, start, [(number(x, shards), half) for x, half in pieces], lefts))
    has_total = total is not None
    tail = tail_rows(rows)

    def kernel(*refs):
        index_refs, refs = refs[:len(indices)], refs[len(indices):]
        if parcels:
            *refs, tables, sems = refs
        out_ref = refs[-1]
        row_at, col_at = lax.axis_index("row"), lax.axis_index("col")

        def run(p):
            chosen = [entry for entry in plan if entry[1] is None or entry[1] == p]
            wanted_parcels = sorted({entry[3] for entry in chosen if entry[2]})
            copies = [
                pltpu.make_async_copy(refs[parcels[n]].at[pl.ds(shards[parcels[n]].shape[0] - tail, tail)], tables.at[n], sems.at[n])
                for n in wanted_parcels
            ]
            for copy in copies:
                copy.start()
            out_ref[...] = refs[-2][...] if has_total else jnp.zeros_like(out_ref)
            for copy in copies:
                copy.wait()

            def tile(n, at):
                return refs[n][pl.ds(pl.multiple_of(at * block, block), block), :]

            def one_row(i, carry):
                wanted = [index_refs[1][i, col_at * outs + o] for o in range(outs)]
                for s in range(slots):
                    half, here = s // slots_dev, s % slots_dev
                    ahead = lax.rem(col_at + half, ncol)
                    k = index_refs[0][i, ahead * slots_dev + here]
                    group, local = lax.div(k, rows), lax.rem(k, rows)
                    offset = lax.rem(group - row_at + nrow, nrow)
                    live = lax.rem(ahead - offset + nrow + nrow, nrow) < WINDOW
                    for d, _, is_parcel, source, start, pieces, lefts in chosen:
                        if half not in lefts:
                            continue

                        @pl.when(live & (offset == d % nrow))
                        def _():
                            found = []
                            for n, piece_half in pieces:
                                for t in range(slots_dev):
                                    slot = lax.rem(col_at + piece_half, ncol) * slots_dev + t
                                    if is_parcel:
                                        column = tables[source, start + local, slot].astype(jnp.int32)
                                    else:
                                        column = index_refs[source][start + local, slot]
                                    found.append((n, t, column))
                            for o in range(outs):
                                matches = [column == wanted[o] for _, _, column in found]

                                @pl.when(functools.reduce(jnp.logical_or, matches))
                                def _():
                                    mixed = 0.0
                                    for match, (n, t, _) in zip(matches, found):
                                        mixed += jnp.where(match, 1.0, 0.0) * tile(n, local * slots_dev + t)
                                    shard = left_at[half]
                                    left_tile = tile(shard[p if len(shard) > 1 else 0], i * slots_dev + here)
                                    left_high, left_low = split(left_tile)
                                    high, low = split(mixed)
                                    dot = functools.partial(jnp.dot, preferred_element_type=jnp.float32)
                                    out_ref[i, o] += dot(left_high, high) + (dot(left_high, low) + dot(left_low, high))

                return carry

            lax.fori_loop(0, rows, one_row, 0)

        by_parity(paired, run)

    operands = shards + ([total] if has_total else [])
    scratch = [pltpu.SMEM((len(parcels), tail, block), jnp.float32), pltpu.SemaphoreType.DMA((len(parcels),))]
    return pl.pallas_call(
        kernel,
        out_shape=jax.ShapeDtypeStruct((rows, outs, block, block), jnp.float32),
        in_specs=[SMEM] * len(indices) + [VMEM] * len(operands),
        out_specs=VMEM,
        scratch_shapes=scratch if parcels else [],
        compiler_params=PARAMS,
        cost_estimate=SOON,
    )(*indices, *operands)


def on_device(p_vals, p_cols, out_cols):
    nrow, ncol = lax.axis_size("row"), lax.axis_size("col")
    rows = p_cols.shape[0]

    def permute(x, source):
        pairs = []
        for r in range(nrow):
            for c in range(ncol):
                if source(r, c) is not None:
                    from_row, from_col = source(r, c)
                    pairs.append((from_row % nrow * ncol + from_col % ncol, r * ncol + c))
        return lax.ppermute(x, ("row", "col"), pairs)

    def after(x, *others):
        return lax.optimization_barrier((x, *others))[0]

    own = p_vals.reshape(-1, p_vals.shape[-1])

    if ncol == 2 and nrow % 2 == 0:
        def by_core(from_even, from_odd):
            return lambda r, c: (from_odd if r % 2 else from_even)(r, c)

        def across(r, c):
            return r, c + 1

        def behind(r, c):
            return r - 2, c

        def ahead(r, c):
            return r + 2, c

        def beside(r, c):
            return r ^ 1, c

        both = (0, 1)
        first = permute(own, by_core(across, behind))
        mate_cols = permute(p_cols, beside)
        beside_own = permute(own, beside)
        total = add_products(p_cols, out_cols, [[own], [own]], [(0, None, (p_cols, 0), [(own, 0)], (0,))], None, True)
        packed = parcel([after(own, beside_own)], [p_cols, mate_cols])
        second = permute(packed, by_core(behind, across))
        third = permute(first, by_core(ahead, across))
        outgoing = parcel([second, beside_own], [mate_cols])
        fourth = permute(outgoing, by_core(across, ahead))
        left = [[own], [first, second]]
        add = functools.partial(add_products, p_cols, out_cols, left)
        total = add(
            [
                (0, 0, (p_cols, 0), [(first, 1)], (0,)),
                (0, 1, (p_cols, 0), [(second, 1)], (0,)),
                (0, 0, (p_cols, 0), [(own, 0), (first, 1)], (1,)),
                (0, 1, (p_cols, 0), [(own, 0), (second, 1)], (1,)),
                (1, 0, (mate_cols, 0), [(beside_own, 0)], both),
                (-1, 1, (mate_cols, 0), [(beside_own, 0)], both),
                (-2, 0, (second, 0), [(second, 0)], both),
            ],
            after(total, outgoing),
            True,
        )
        beside_first = permute(after(first, total), beside)
        beside_second = permute(after(second, total), beside)
        beside_third = permute(third, beside)
        fourth_cols = index_tile(fourth, own.shape[0])
        return add(
            [
                (1, 0, (mate_cols, 0), [(beside_second, 1)], both),
                (-1, 1, (mate_cols, 0), [(beside_first, 1)], both),
                (-2, 0, (second, 0), [(fourth, 1)], both),
                (-2, 1, (beside_second, rows), [(first, 0), (third, 1)], both),
                (-1, 0, (second, rows), [(beside_first, 0), (beside_third, 1)], both),
                (1, 1, (fourth_cols, 0), [(fourth, 0), (beside_third, 1)], both),
            ],
            total,
            True,
        )

    left = [[own]] + [[permute(own, lambda r, c, j=j: (r, c + j))] for j in range(1, ncol)]
    halves = tuple(range(ncol))
    shards, cols = {0: own}, {0: p_cols}
    for d in range(1 - WINDOW, ncol):
        if d:
            shards[d], cols[d] = (permute(x, lambda r, c, d=d: (r + d, c)) for x in (own, p_cols))
    total = None
    for j in halves:
        layer = {d: permute(x, lambda r, c, j=j: (r, c + j)) if j else x for d, x in shards.items()}
        entries = [(d, None, (cols[d], 0), [(x, j)], halves) for d, x in layer.items()]
        total = add_products(p_cols, out_cols, left, entries, total, False)
    return total


def solution(mesh):
    placed = (P("row", "col", None, None), P("row", None), P("row", None))
    return jax.shard_map(
        on_device,
        mesh=mesh,
        in_specs=placed,
        out_specs=P("row", "col", None, None),
        check_vma=False,
    )
```

```python
import functools

import jax
import jax.numpy as jnp
from jax import lax
from jax.experimental import pallas as pl
from jax.experimental.pallas import tpu as pltpu
from jax.sharding import PartitionSpec as P

WINDOW = 3
SUBLANES = 8
SMEM = pl.BlockSpec(memory_space=pltpu.SMEM)
VMEM = pl.BlockSpec(memory_space=pltpu.VMEM)
PARAMS = pltpu.CompilerParams(vmem_limit_bytes=48 * 2**20)
SOON = pl.CostEstimate(flops=0, bytes_accessed=0, transcendentals=0)


def split(x):
    high = x.astype(jnp.bfloat16)
    return high, (x - high.astype(jnp.float32)).astype(jnp.bfloat16)


def product(left, right):
    left_high, left_low = split(left)
    right_high, right_low = split(right)
    return jnp.dot(
        jnp.concatenate([left_high, left_low, left_high], axis=1),
        jnp.concatenate([right_high, right_high, right_low], axis=0),
        preferred_element_type=jnp.float32,
    )


def tail_rows(rows):
    return -(-2 * rows // SUBLANES) * SUBLANES


def by_parity(paired, run):
    if paired:
        parity = lax.rem(lax.axis_index("row"), 2)
        pl.when(parity == 0)(lambda: run(0))
        pl.when(parity == 1)(lambda: run(1))
    else:
        run(None)


def pack(blocks, tables, *ahead):
    tall, block = blocks.shape
    rows, slots = tables[0].shape
    tail = tail_rows(rows)

    def kernel(*refs):
        cols_refs, blocks_ref, (out_ref, sem) = refs[:len(tables)], refs[len(tables)], refs[-2:]
        copy = pltpu.make_async_copy(blocks_ref, out_ref.at[pl.ds(0, tall)], sem)
        copy.start()
        row, column = (lax.broadcasted_iota(jnp.int32, (tail, block), d) for d in (0, 1))
        cols = jnp.zeros((tail, block), jnp.float32)
        for n, ref in enumerate(cols_refs):
            for r in range(rows):
                for s in range(slots):
                    here = (row == n * rows + r) & (column == s)
                    cols = jnp.where(here, ref[r, s], cols)
        out_ref[pl.ds(tall, tail)] = cols
        copy.wait()

    return pl.pallas_call(
        kernel,
        out_shape=jax.ShapeDtypeStruct((tall + tail, block), jnp.float32),
        in_specs=[SMEM] * len(tables) + [VMEM] * (1 + len(ahead)),
        out_specs=VMEM,
        scratch_shapes=[pltpu.SemaphoreType.DMA],
        compiler_params=PARAMS,
        cost_estimate=SOON,
    )(*tables, blocks, *ahead)


def repack(tall, even, odd, *ahead):
    def kernel(*refs):
        out_ref, sems = refs[-2:]

        def run(p):
            copies = [
                pltpu.make_async_copy(refs[2 * p].at[pl.ds(0, tall)], out_ref.at[pl.ds(0, tall)], sems.at[0]),
                pltpu.make_async_copy(refs[2 * p + 1].at[pl.ds(tall, tail)], out_ref.at[pl.ds(tall, tail)], sems.at[1]),
            ]
            for copy in copies:
                copy.start()
            for copy in copies:
                copy.wait()

        by_parity(True, run)

    tail = even[1].shape[0] - tall
    return pl.pallas_call(
        kernel,
        out_shape=jax.ShapeDtypeStruct(even[1].shape, jnp.float32),
        in_specs=[VMEM] * (4 + len(ahead)),
        out_specs=VMEM,
        scratch_shapes=[pltpu.SemaphoreType.DMA((2,))],
        compiler_params=PARAMS,
        cost_estimate=SOON,
    )(*even, *odd, *ahead)


def list_pairs(p_cols, ncol, offsets):
    rows, slots = p_cols.shape
    slots_dev = slots // ncol
    nrow = lax.axis_size("row")
    heads, cap = ncol * len(offsets), rows * slots_dev

    def kernel(p_cols_ref, out_ref):
        row_at, col_at = lax.axis_index("row"), lax.axis_index("col")
        for n in range(heads):
            out_ref[n] = 0

        def one_row(i, carry):
            for s in range(slots):
                half, here = s // slots_dev, s % slots_dev
                ahead = lax.rem(col_at + half, ncol)
                k = p_cols_ref[i, ahead * slots_dev + here]
                group, local = lax.div(k, rows), lax.rem(k, rows)
                steps = lax.rem(row_at + ahead - group + nrow, nrow)

                @pl.when(steps < WINDOW)
                def _():
                    head = half * len(offsets) + ahead - steps + WINDOW - 1
                    long = out_ref[head]
                    out_ref[heads + head * cap + long] = (i * slots_dev + here) * rows + local
                    out_ref[head] = long + 1

            return carry

        lax.fori_loop(0, rows, one_row, 0)

    return pl.pallas_call(
        kernel,
        out_shape=jax.ShapeDtypeStruct((heads * (cap + 1),), jnp.int32),
        in_specs=[SMEM],
        out_specs=SMEM,
        compiler_params=PARAMS,
        cost_estimate=SOON,
    )(p_cols)


def index_tile(source, tall, flops, *ahead):
    def kernel(source_ref, *refs):
        out_ref, sem = refs[-2:]
        copy = pltpu.make_async_copy(source_ref.at[pl.ds(tall, out_ref.shape[0])], out_ref, sem)
        copy.start()
        copy.wait()

    return pl.pallas_call(
        kernel,
        out_shape=jax.ShapeDtypeStruct((source.shape[0] - tall, source.shape[1]), jnp.float32),
        in_specs=[VMEM] * (1 + len(ahead)),
        out_specs=VMEM,
        scratch_shapes=[pltpu.SemaphoreType.DMA],
        compiler_params=PARAMS,
        cost_estimate=pl.CostEstimate(flops=flops, bytes_accessed=0, transcendentals=0),
    )(source, *ahead)


def add_products(pairs, offsets, out_cols, left, entries, total, paired, last=False):
    ncol = len(left)
    outs = out_cols.shape[1] // ncol
    block = left[0][0].shape[1]
    rows = out_cols.shape[0]
    slots_dev = out_cols.shape[1] // ncol
    heads, cap = ncol * len(offsets), rows * slots_dev
    shards, indices = [], [pairs, out_cols.astype(jnp.float32)]

    def number(array, known):
        for n, x in enumerate(known):
            if x is array:
                return n
        known.append(array)
        return len(known) - 1

    left_at = [[number(x, shards) for x in part] for part in left]
    plan = [
        (offsets.index(d), p, number(cols, indices), start, [(number(x, shards), half) for x, half in pieces], lefts)
        for d, p, (cols, start), pieces, lefts in entries
    ]
    has_total = total is not None

    def kernel(*refs):
        index_refs, refs = refs[:len(indices)], refs[len(indices):]
        if last:
            total_ref, out_ref, sums, sem = refs[-4:]
            copy = pltpu.make_async_copy(total_ref, sums, sem)
            copy.start()
            copy.wait()
        else:
            sums = refs[-1]
            sums[...] = refs[-2][...] if has_total else jnp.zeros_like(sums)
        col_at = lax.axis_index("col")

        def tile(n, at):
            return refs[n][pl.ds(pl.multiple_of(at * block, block), block), :]

        def run(p):
            for n, q, source, start, pieces, lefts in plan:
                if q is not None and q != p:
                    continue
                for half in lefts:
                    head = half * len(offsets) + n
                    left_shard = left_at[half][p if len(left_at[half]) > 1 else 0]

                    def one_pair(m, carry):
                        pair = index_refs[0][heads + head * cap + m]
                        here, local = lax.div(pair, rows), lax.rem(pair, rows)
                        i = lax.div(here, slots_dev)
                        wanted = [index_refs[1][i, col_at * outs + o] for o in range(outs)]
                        found = []
                        for shard, piece_half in pieces:
                            for t in range(slots_dev):
                                column = index_refs[source][start + local, lax.rem(col_at + piece_half, ncol) * slots_dev + t]
                                found += [(column == wanted[o], shard, t, o) for o in range(outs)]

                        @pl.when(functools.reduce(jnp.logical_or, [match for match, *_ in found]))
                        def _():
                            for match, shard, t, o in found:

                                @pl.when(match)
                                def _():
                                    sums[i, o] += product(tile(left_shard, here), tile(shard, local * slots_dev + t))

                        return carry

                    lax.fori_loop(0, index_refs[0][head], one_pair, 0)

        by_parity(paired, run)
        if last:
            copy = pltpu.make_async_copy(sums, out_ref, sem)
            copy.start()
            copy.wait()

    operands = shards + ([total] if has_total else [])
    shape = (rows, outs, block, block)
    return pl.pallas_call(
        kernel,
        out_shape=jax.ShapeDtypeStruct(shape, jnp.float32),
        in_specs=[SMEM] * len(indices) + [VMEM] * len(operands),
        out_specs=pl.BlockSpec(memory_space=pltpu.HBM) if last else VMEM,
        scratch_shapes=[pltpu.VMEM(shape, jnp.float32), pltpu.SemaphoreType.DMA] if last else [],
        compiler_params=PARAMS,
        cost_estimate=SOON,
    )(*indices, *operands)


def on_device(p_vals, p_cols, out_cols):
    nrow, ncol = lax.axis_size("row"), lax.axis_size("col")
    rows = p_cols.shape[0]

    def permute(x, source):
        pairs = []
        for r in range(nrow):
            for c in range(ncol):
                if source(r, c) is not None:
                    from_row, from_col = source(r, c)
                    pairs.append((from_row % nrow * ncol + from_col % ncol, r * ncol + c))
        return lax.ppermute(x, ("row", "col"), pairs)

    def after(x, *others):
        return lax.optimization_barrier((x, *others))[0]

    own = p_vals.reshape(-1, p_vals.shape[-1])
    offsets = tuple(range(1 - WINDOW, ncol))
    pairs = list_pairs(p_cols, ncol, offsets)

    if ncol == 2 and nrow % 2 == 0:
        def by_core(from_even, from_odd):
            return lambda r, c: (from_odd if r % 2 else from_even)(r, c)

        def across(r, c):
            return r, c + 1

        def behind(r, c):
            return r - 2, c

        def ahead(r, c):
            return r + 2, c

        def beside(r, c):
            return r ^ 1, c

        both = (0, 1)
        tall = own.shape[0]
        first = permute(own, by_core(across, behind))
        own_cols = p_cols.astype(jnp.float32)
        mate_cols = permute(own_cols, beside)
        beside_own = permute(own, beside)
        packed = pack(own, [own_cols, mate_cols], beside_own)
        second = permute(packed, by_core(behind, across))
        next_first = permute(first, lambda r, c: (r + 1, c))
        third = permute(first, lambda r, c: (r, c + 1) if r % 2 else None)
        outgoing = repack(tall, (second, second), (beside_own, packed))
        fourth = permute(outgoing, by_core(across, ahead))
        left = [[packed], [first, second]]

        def add(entries, total, last=False):
            return add_products(pairs, offsets, out_cols, left, entries, total, True, last)

        back_cols = index_tile(second, tall, 0, outgoing)
        total = add(
            [
                (0, 0, (own_cols, 0), [(packed, 0), (first, 1)], both),
                (0, 1, (own_cols, 0), [(packed, 0), (second, 1)], both),
                (1, 0, (mate_cols, 0), [(beside_own, 0)], both),
                (-1, 1, (mate_cols, 0), [(beside_own, 0)], both),
                (-2, 0, (back_cols, 0), [(second, 0)], both),
            ],
            None,
        )
        beside_other = permute(repack(tall, (first, second), (second, second), total), beside)
        beside_third = permute(third, lambda r, c: None if r % 2 else (r + 1, c))
        late_cols = index_tile(second, tall, 10**9, next_first)
        far_cols = index_tile(fourth, tall, 10**9, late_cols)
        mate_back_cols = index_tile(beside_other, tall, 0, far_cols)
        return add(
            [
                (1, 0, (mate_cols, 0), [(beside_other, 1)], both),
                (-1, 1, (mate_cols, 0), [(beside_other, 1)], both),
                (-2, 0, (late_cols, 0), [(fourth, 1)], both),
                (-2, 1, (mate_back_cols, rows), [(first, 0), (third, 1)], both),
                (-1, 0, (late_cols, rows), [(next_first, 0), (beside_third, 1)], both),
                (1, 1, (far_cols, rows), [(fourth, 0), (next_first, 1)], both),
            ],
            total,
            True,
        )

    left = [[own]] + [[permute(own, lambda r, c, j=j: (r, c + j))] for j in range(1, ncol)]
    halves = tuple(range(ncol))
    own_cols = p_cols.astype(jnp.float32)
    shards, cols = {0: own}, {0: own_cols}
    for d in offsets:
        if d:
            shards[d], cols[d] = (permute(x, lambda r, c, d=d: (r + d, c)) for x in (own, own_cols))
    total = None
    for j in halves:
        layer = {d: permute(x, lambda r, c, j=j: (r, c + j)) if j else x for d, x in shards.items()}
        entries = [(d, None, (cols[d], 0), [(x, j)], halves) for d, x in layer.items()]
        total = add_products(pairs, offsets, out_cols, left, entries, total, False)
    return total


def solution(mesh):
    placed = (P("row", "col", None, None), P("row", None), P("row", None))
    return jax.shard_map(
        on_device,
        mesh=mesh,
        in_specs=placed,
        out_specs=P("row", "col", None, None),
        check_vma=False,
    )
```

```python
import functools

import jax
import jax.numpy as jnp
from jax import lax
from jax.experimental import pallas as pl
from jax.experimental.pallas import tpu as pltpu
from jax.sharding import PartitionSpec as P

WINDOW = 3
TOGETHER = 4
SUBLANES = 8
SMEM = pl.BlockSpec(memory_space=pltpu.SMEM)
VMEM = pl.BlockSpec(memory_space=pltpu.VMEM)
PARAMS = pltpu.CompilerParams(vmem_limit_bytes=48 * 2**20)
SOON = pl.CostEstimate(flops=0, bytes_accessed=0, transcendentals=0)


def split(x):
    high = x.astype(jnp.bfloat16)
    return high, (x - high.astype(jnp.float32)).astype(jnp.bfloat16)


def product(left, right):
    left_high, left_low = split(left)
    right_high, right_low = split(right)
    return jnp.dot(
        jnp.concatenate([left_high, left_low, left_high], axis=1),
        jnp.concatenate([right_high, right_high, right_low], axis=0),
        preferred_element_type=jnp.float32,
    )


def by_parity(paired, run):
    if paired:
        parity = lax.rem(lax.axis_index("row"), 2)
        pl.when(parity == 0)(lambda: run(0))
        pl.when(parity == 1)(lambda: run(1))
    else:
        run(None)


def pack(blocks, tables, *ahead):
    tall, block = blocks.shape
    rows, slots = tables[0].shape
    tail = SUBLANES

    def kernel(*refs):
        cols_refs, blocks_ref, (out_ref, sem) = refs[:len(tables)], refs[len(tables)], refs[-2:]
        copy = pltpu.make_async_copy(blocks_ref, out_ref.at[pl.ds(0, tall)], sem)
        copy.start()
        row, column = (lax.broadcasted_iota(jnp.int32, (tail, block), d) for d in (0, 1))
        cols = jnp.zeros((tail, block), jnp.float32)
        for n, ref in enumerate(cols_refs):
            for r in range(rows):
                for s in range(slots):
                    here = (row == r) & (column == n * slots + s)
                    cols = jnp.where(here, ref[r, s], cols)
        out_ref[pl.ds(tall, tail)] = cols
        copy.wait()

    return pl.pallas_call(
        kernel,
        out_shape=jax.ShapeDtypeStruct((tall + tail, block), jnp.float32),
        in_specs=[SMEM] * len(tables) + [VMEM] * (1 + len(ahead)),
        out_specs=VMEM,
        scratch_shapes=[pltpu.SemaphoreType.DMA],
        compiler_params=PARAMS,
        cost_estimate=SOON,
    )(*tables, blocks, *ahead)


def repack(tall, even, odd, *ahead):
    def kernel(*refs):
        out_ref, sems = refs[-2:]

        def run(p):
            copies = [
                pltpu.make_async_copy(refs[2 * p].at[pl.ds(0, tall)], out_ref.at[pl.ds(0, tall)], sems.at[0]),
                pltpu.make_async_copy(refs[2 * p + 1].at[pl.ds(tall, tail)], out_ref.at[pl.ds(tall, tail)], sems.at[1]),
            ]
            for copy in copies:
                copy.start()
            for copy in copies:
                copy.wait()

        by_parity(True, run)

    tail = even[1].shape[0] - tall
    return pl.pallas_call(
        kernel,
        out_shape=jax.ShapeDtypeStruct(even[1].shape, jnp.float32),
        in_specs=[VMEM] * (4 + len(ahead)),
        out_specs=VMEM,
        scratch_shapes=[pltpu.SemaphoreType.DMA((2,))],
        compiler_params=PARAMS,
        cost_estimate=SOON,
    )(*even, *odd, *ahead)


def stack(tall, even, odd):
    def kernel(*refs):
        out_ref, sems = refs[-2:]

        def run(p):
            copies = [
                pltpu.make_async_copy(refs[2 * p + n].at[pl.ds(0, tall)], out_ref.at[pl.ds(n * tall, tall)], sems.at[n])
                for n in range(2)
            ]
            for copy in copies:
                copy.start()
            for copy in copies:
                copy.wait()

        by_parity(True, run)

    return pl.pallas_call(
        kernel,
        out_shape=jax.ShapeDtypeStruct((2 * tall, even[0].shape[1]), jnp.float32),
        in_specs=[VMEM] * 4,
        out_specs=VMEM,
        scratch_shapes=[pltpu.SemaphoreType.DMA((2,))],
        compiler_params=PARAMS,
        cost_estimate=SOON,
    )(*even, *odd)


def beside_each_other(rows, width, *tiles):
    arrays = [x for pair in tiles for x in pair]

    def kernel(*refs):
        out_ref = refs[-1]

        def run(p):
            shape = (SUBLANES, arrays[0].shape[1])
            column = lax.broadcasted_iota(jnp.int32, shape, 1)
            result = jnp.zeros(shape, jnp.float32)
            for n in range(len(tiles)):
                ref, tall = refs[2 * n + p], arrays[2 * n + p].shape[0] - SUBLANES
                moved = ref[pl.ds(tall, SUBLANES), :]
                moved = pltpu.roll(moved, n * width, 1) if n else moved
                result = jnp.where((column >= n * width) & (column < (n + 1) * width), moved, result)
            out_ref[...] = result[:out_ref.shape[0], :out_ref.shape[1]]

        by_parity(True, run)

    return pl.pallas_call(
        kernel,
        out_shape=jax.ShapeDtypeStruct((rows, len(tiles) * width), jnp.float32),
        in_specs=[VMEM] * len(arrays),
        out_specs=VMEM,
        compiler_params=PARAMS,
        cost_estimate=SOON,
    )(*arrays)


def list_pairs(p_cols, ncol, offsets):
    rows, slots = p_cols.shape
    slots_dev = slots // ncol
    nrow = lax.axis_size("row")
    heads, cap = ncol * len(offsets), rows * slots_dev

    def kernel(p_cols_ref, out_ref):
        row_at, col_at = lax.axis_index("row"), lax.axis_index("col")
        for n in range(heads):
            out_ref[n, cap] = 0

        def one_row(i, carry):
            for s in range(slots):
                half, here = s // slots_dev, s % slots_dev
                ahead = lax.rem(col_at + half, ncol)
                k = p_cols_ref[i, ahead * slots_dev + here]
                group, local = lax.div(k, rows), lax.rem(k, rows)
                steps = lax.rem(row_at + ahead - group + nrow, nrow)

                @pl.when(steps < WINDOW)
                def _():
                    head = half * len(offsets) + ahead - steps + WINDOW - 1
                    long = out_ref[head, cap]
                    out_ref[head, long] = (i * slots_dev + here) * rows + local
                    out_ref[head, cap] = long + 1

            return carry

        lax.fori_loop(0, rows, one_row, 0)

    return pl.pallas_call(
        kernel,
        out_shape=jax.ShapeDtypeStruct((heads, cap + 1), jnp.int32),
        in_specs=[SMEM],
        out_specs=SMEM,
        compiler_params=PARAMS,
        cost_estimate=SOON,
    )(p_cols)


def index_tile(source, tall, flops, *ahead):
    def kernel(source_ref, *refs):
        out_ref, sem = refs[-2:]
        copy = pltpu.make_async_copy(source_ref.at[pl.ds(tall, out_ref.shape[0])], out_ref, sem)
        copy.start()
        copy.wait()

    return pl.pallas_call(
        kernel,
        out_shape=jax.ShapeDtypeStruct((source.shape[0] - tall, source.shape[1]), jnp.float32),
        in_specs=[VMEM] * (1 + len(ahead)),
        out_specs=VMEM,
        scratch_shapes=[pltpu.SemaphoreType.DMA],
        compiler_params=PARAMS,
        cost_estimate=pl.CostEstimate(flops=flops, bytes_accessed=0, transcendentals=0),
    )(source, *ahead)


def add_products(pairs, offsets, out_cols, left, entries, total, paired):
    ncol = len(left)
    outs = out_cols.shape[1] // ncol
    block = left[0][0].shape[1]
    rows = out_cols.shape[0]
    slots_dev = out_cols.shape[1] // ncol
    cap = rows * slots_dev
    shards, indices = [], [pairs, out_cols.astype(jnp.float32)]

    def number(array, known):
        for n, x in enumerate(known):
            if x is array:
                return n
        known.append(array)
        return len(known) - 1

    left_at = [[number(x, shards) for x in part] for part in left]
    plan = [
        (offsets.index(d), p, number(cols, indices), start, [(number(x, shards), half) for x, half in pieces], lefts)
        for d, p, (cols, start), pieces, lefts in entries
    ]
    has_total = total is not None

    def kernel(*refs):
        index_refs, refs = refs[:len(indices)], refs[len(indices):]
        sums = refs[-1]
        sums[...] = refs[-2][...] if has_total else jnp.zeros_like(sums)
        col_at = lax.axis_index("col")

        def tile(n, at):
            return refs[n][pl.ds(pl.multiple_of(at * block, block), block), :]

        def run(p):
            for n, q, source, start, pieces, lefts in plan:
                if q is not None and q != p:
                    continue
                for half in lefts:
                    head = half * len(offsets) + n
                    left_shard = left_at[half][p if len(left_at[half]) > 1 else 0]

                    def one_pair(m, carry):
                        pair = index_refs[0][head, m]
                        here, local = lax.div(pair, rows), lax.rem(pair, rows)
                        i = lax.div(here, slots_dev)
                        wanted = [index_refs[1][i, col_at * outs + o] for o in range(outs)]
                        found = []
                        for shard, piece_half in pieces:
                            for t in range(slots_dev):
                                column = index_refs[source][local, start + lax.rem(col_at + piece_half, ncol) * slots_dev + t]
                                found += [(column == wanted[o], shard, t, o) for o in range(outs)]

                        @pl.when(functools.reduce(jnp.logical_or, [match for match, *_ in found]))
                        def _():
                            for match, shard, t, o in found:

                                @pl.when(match)
                                def _():
                                    sums[i, o] += product(tile(left_shard, here), tile(shard, local * slots_dev + t))

                        return carry

                    lax.fori_loop(0, index_refs[0][head, cap], one_pair, 0)

        by_parity(paired, run)

    operands = shards + ([total] if has_total else [])
    shape = (rows, outs, block, block)
    return pl.pallas_call(
        kernel,
        out_shape=jax.ShapeDtypeStruct(shape, jnp.float32),
        in_specs=[SMEM] * len(indices) + [VMEM] * len(operands),
        out_specs=VMEM,
        compiler_params=PARAMS,
        cost_estimate=SOON,
    )(*indices, *operands)


def finish(pairs, offsets, tables, wanted_at, left, rights, entries, total):
    rows, outs, block = total.shape[:3]
    nright = max(len(part) for part in rights)
    slots_dev = outs
    ncol = left.shape[0] // (rows * slots_dev * block)
    blocks = rows * slots_dev
    tall = blocks * block
    cap = blocks
    targets = rows * outs
    longest = ncol * blocks * outs * slots_dev * max(sum(len(pieces) for *_, pieces in part) for part in entries)
    shards, indices = [left], [pairs, tables]

    def number(array, known):
        for n, x in enumerate(known):
            if x is array:
                return n
        known.append(array)
        return len(known) - 1

    rights_at = [[number(x, shards) for x in part] for part in rights]
    plan = [[(offsets.index(d), start, pieces) for d, start, pieces in part] for part in entries]

    def kernel(*refs):
        brought, refs = refs[:len(indices)], refs[len(indices):]
        total_ref, out_ref, right, sums, listed, sems, index_sems = refs[len(shards):len(shards) + 7]
        index_refs = refs[len(shards) + 7:]
        index_copies = [pltpu.make_async_copy(x, y, index_sems.at[n]) for n, (x, y) in enumerate(zip(brought, index_refs))]
        for copy in index_copies:
            copy.start()
        lefts = refs[0]
        pairs_ref, tables_ref = index_refs
        col_at = lax.axis_index("col")

        def run(p):
            copies = [
                pltpu.make_async_copy(refs[n].at[pl.ds(0, tall)], right.at[pl.ds(m * tall, tall)], sems.at[m])
                for m, n in enumerate(rights_at[p])
            ]
            copies.append(pltpu.make_async_copy(total_ref, sums.at[pl.ds(0, targets)], sems.at[nright]))
            for copy in copies:
                copy.start()

            for copy in index_copies:
                copy.wait()
            long = jnp.int32(0)
            for n, start, pieces in plan[p]:
                for half in range(ncol):
                    head = half * len(offsets) + n

                    def one_pair(m, long):
                        pair = pairs_ref[head, m]
                        here, local = lax.div(pair, rows), lax.rem(pair, rows)
                        i = lax.div(here, slots_dev)
                        for shard, piece_half in pieces:
                            for t in range(slots_dev):
                                column = tables_ref[local, start + lax.rem(col_at + piece_half, ncol) * slots_dev + t]
                                code = (half * blocks + here) * nright * blocks + shard * blocks + local * slots_dev + t
                                for o in range(outs):
                                    listed[long] = code * targets + i * outs + o
                                    long += (column == tables_ref[i, wanted_at + col_at * outs + o]).astype(jnp.int32)
                        return long

                    long = lax.fori_loop(0, pairs_ref[head, cap], one_pair, long)
            for copy in copies:
                copy.wait()

            def tile(ref, at):
                return ref[pl.ds(pl.multiple_of(at * block, block), block), :]

            def some(m, carry):
                found = []
                for n in range(TOGETHER):
                    at = m * TOGETHER + n
                    code = listed[jnp.minimum(at, long - 1)]
                    tiles, target = lax.div(code, targets), lax.rem(code, targets)
                    result = product(tile(lefts, lax.div(tiles, nright * blocks)), tile(right, lax.rem(tiles, nright * blocks)))
                    found.append((jnp.where(at < long, target, targets), result))
                for target, result in found:
                    sums[target] += result
                return carry

            lax.fori_loop(0, lax.div(long + TOGETHER - 1, TOGETHER), some, 0)

        by_parity(True, run)
        copy = pltpu.make_async_copy(sums.at[pl.ds(0, targets)], out_ref, sems.at[0])
        copy.start()
        copy.wait()

    result = pl.pallas_call(
        kernel,
        out_shape=jax.ShapeDtypeStruct((targets, block, block), jnp.float32),
        in_specs=[VMEM] * (len(indices) + len(shards) + 1),
        out_specs=pl.BlockSpec(memory_space=pltpu.HBM),
        scratch_shapes=[
            pltpu.VMEM((nright * tall, block), jnp.float32),
            pltpu.VMEM((targets + 1, block, block), jnp.float32),
            pltpu.SMEM((longest + 1,), jnp.int32),
            pltpu.SemaphoreType.DMA((nright + 1,)),
            pltpu.SemaphoreType.DMA((len(indices),)),
        ]
        + [pltpu.SMEM(x.shape, x.dtype) for x in indices],
        compiler_params=PARAMS,
        cost_estimate=SOON,
    )(*indices, *shards, total.reshape(targets, block, block))
    return result.reshape(total.shape)


def on_device(p_vals, p_cols, out_cols):
    nrow, ncol = lax.axis_size("row"), lax.axis_size("col")
    rows = p_cols.shape[0]

    def permute(x, source):
        pairs = []
        for r in range(nrow):
            for c in range(ncol):
                if source(r, c) is not None:
                    from_row, from_col = source(r, c)
                    pairs.append((from_row % nrow * ncol + from_col % ncol, r * ncol + c))
        return lax.ppermute(x, ("row", "col"), pairs)

    def after(x, *others):
        return lax.optimization_barrier((x, *others))[0]

    own = p_vals.reshape(-1, p_vals.shape[-1])
    offsets = tuple(range(1 - WINDOW, ncol))
    pairs = list_pairs(p_cols, ncol, offsets)

    if ncol == 2 and nrow % 2 == 0 and rows <= SUBLANES and 9 * p_cols.shape[1] <= own.shape[1]:
        def by_core(from_even, from_odd):
            return lambda r, c: (from_odd if r % 2 else from_even)(r, c)

        def across(r, c):
            return r, c + 1

        def behind(r, c):
            return r - 2, c

        def ahead(r, c):
            return r + 2, c

        def beside(r, c):
            return r ^ 1, c

        both = (0, 1)
        tall = own.shape[0]
        first = permute(own, by_core(across, behind))
        own_cols = p_cols.astype(jnp.float32)
        mate_cols = permute(own_cols, beside)
        beside_own = permute(own, beside)
        packed = pack(own, [own_cols, mate_cols, out_cols.astype(jnp.float32)], beside_own)
        second = permute(packed, by_core(behind, across))
        next_first = permute(first, lambda r, c: (r + 1, c))
        third = permute(first, lambda r, c: (r, c + 1) if r % 2 else None)
        outgoing = repack(tall, (second, second), (beside_own, packed))
        fourth = permute(outgoing, by_core(across, ahead))
        left = [[packed], [first, second]]

        back_cols = index_tile(second, tall, 0, outgoing)
        total = add_products(
            pairs,
            offsets,
            out_cols,
            left,
            [
                (0, 0, (own_cols, 0), [(packed, 0), (first, 1)], both),
                (0, 1, (own_cols, 0), [(packed, 0), (second, 1)], both),
                (1, 0, (mate_cols, 0), [(beside_own, 0)], both),
                (-1, 1, (mate_cols, 0), [(beside_own, 0)], both),
                (-2, 0, (back_cols, 0), [(second, 0)], both),
            ],
            None,
            True,
        )
        beside_other = permute(repack(tall, (first, second), (second, second), total), beside)
        beside_third = permute(third, lambda r, c: None if r % 2 else (r + 1, c))
        late_cols = index_tile(second, tall, 10**9, next_first)
        far_cols = index_tile(fourth, tall, 10**9, late_cols)
        width = 3 * p_cols.shape[1]
        own_at, mate_at, wanted_at = (n * p_cols.shape[1] for n in range(3))
        tables = beside_each_other(rows, width, (packed, packed), (late_cols, beside_other), (far_cols, far_cols))
        return finish(
            pairs,
            offsets,
            tables,
            wanted_at,
            stack(tall, (packed, first), (packed, second)),
            [[beside_other, fourth, next_first, beside_third], [beside_other, first, third, fourth, next_first]],
            [
                [
                    (1, mate_at, [(0, 1)]),
                    (-2, width + own_at, [(1, 1)]),
                    (-1, width + mate_at, [(2, 0), (3, 1)]),
                ],
                [
                    (-1, mate_at, [(0, 1)]),
                    (-2, width + mate_at, [(1, 0), (2, 1)]),
                    (1, 2 * width + mate_at, [(3, 0), (4, 1)]),
                ],
            ],
            total,
        )

    left = [[own]] + [[permute(own, lambda r, c, j=j: (r, c + j))] for j in range(1, ncol)]
    halves = tuple(range(ncol))
    own_cols = p_cols.astype(jnp.float32)
    shards, cols = {0: own}, {0: own_cols}
    for d in offsets:
        if d:
            shards[d], cols[d] = (permute(x, lambda r, c, d=d: (r + d, c)) for x in (own, own_cols))
    total = None
    for j in halves:
        layer = {d: permute(x, lambda r, c, j=j: (r, c + j)) if j else x for d, x in shards.items()}
        entries = [(d, None, (cols[d], 0), [(x, j)], halves) for d, x in layer.items()]
        total = add_products(pairs, offsets, out_cols, left, entries, total, False)
    return total


def solution(mesh):
    placed = (P("row", "col", None, None), P("row", None), P("row", None))
    return jax.shard_map(
        on_device,
        mesh=mesh,
        in_specs=placed,
        out_specs=P("row", "col", None, None),
        check_vma=False,
    )
```

```python
import functools

import jax
import jax.numpy as jnp
from jax import lax
from jax.experimental import pallas as pl
from jax.experimental.pallas import tpu as pltpu
from jax.sharding import PartitionSpec as P

WINDOW = 3
TOGETHER = 4
SUBLANES = 8
SMEM = pl.BlockSpec(memory_space=pltpu.SMEM)
VMEM = pl.BlockSpec(memory_space=pltpu.VMEM)
PARAMS = pltpu.CompilerParams(vmem_limit_bytes=48 * 2**20)
SOON = pl.CostEstimate(flops=0, bytes_accessed=0, transcendentals=0)


def split(x):
    high = x.astype(jnp.bfloat16)
    return high, (x - high.astype(jnp.float32)).astype(jnp.bfloat16)


def product(left, right):
    left_high, left_low = split(left)
    right_high, right_low = split(right)
    return jnp.dot(
        jnp.concatenate([left_high, left_low, left_high], axis=1),
        jnp.concatenate([right_high, right_high, right_low], axis=0),
        preferred_element_type=jnp.float32,
    )


def by_parity(paired, run):
    if paired:
        parity = lax.rem(lax.axis_index("row"), 2)
        pl.when(parity == 0)(lambda: run(0))
        pl.when(parity == 1)(lambda: run(1))
    else:
        run(None)


def pack(blocks, tables, *ahead):
    tall, block = blocks.shape
    rows, slots = tables[0].shape
    tail = SUBLANES

    def kernel(*refs):
        cols_refs, blocks_ref, (out_ref, sem) = refs[:len(tables)], refs[len(tables)], refs[-2:]
        copy = pltpu.make_async_copy(blocks_ref, out_ref.at[pl.ds(0, tall)], sem)
        copy.start()
        row, column = (lax.broadcasted_iota(jnp.int32, (tail, block), d) for d in (0, 1))
        cols = jnp.zeros((tail, block), jnp.float32)
        for n, ref in enumerate(cols_refs):
            for r in range(rows):
                for s in range(slots):
                    here = (row == r) & (column == n * slots + s)
                    cols = jnp.where(here, ref[r, s], cols)
        out_ref[pl.ds(tall, tail)] = cols
        copy.wait()

    return pl.pallas_call(
        kernel,
        out_shape=jax.ShapeDtypeStruct((tall + tail, block), jnp.float32),
        in_specs=[SMEM] * len(tables) + [VMEM] * (1 + len(ahead)),
        out_specs=VMEM,
        scratch_shapes=[pltpu.SemaphoreType.DMA],
        compiler_params=PARAMS,
        cost_estimate=SOON,
    )(*tables, blocks, *ahead)


def repack(tall, even, odd, *ahead):
    def kernel(*refs):
        out_ref, sems = refs[-2:]

        def run(p):
            copies = [
                pltpu.make_async_copy(refs[2 * p].at[pl.ds(0, tall)], out_ref.at[pl.ds(0, tall)], sems.at[0]),
                pltpu.make_async_copy(refs[2 * p + 1].at[pl.ds(tall, tail)], out_ref.at[pl.ds(tall, tail)], sems.at[1]),
            ]
            for copy in copies:
                copy.start()
            for copy in copies:
                copy.wait()

        by_parity(True, run)

    tail = even[1].shape[0] - tall
    return pl.pallas_call(
        kernel,
        out_shape=jax.ShapeDtypeStruct(even[1].shape, jnp.float32),
        in_specs=[VMEM] * (4 + len(ahead)),
        out_specs=VMEM,
        scratch_shapes=[pltpu.SemaphoreType.DMA((2,))],
        compiler_params=PARAMS,
        cost_estimate=SOON,
    )(*even, *odd, *ahead)


def stack(tall, even, odd):
    def kernel(*refs):
        out_ref, sems = refs[-2:]

        def run(p):
            copies = [
                pltpu.make_async_copy(refs[2 * p + n].at[pl.ds(0, tall)], out_ref.at[pl.ds(n * tall, tall)], sems.at[n])
                for n in range(2)
            ]
            for copy in copies:
                copy.start()
            for copy in copies:
                copy.wait()

        by_parity(True, run)

    return pl.pallas_call(
        kernel,
        out_shape=jax.ShapeDtypeStruct((2 * tall, even[0].shape[1]), jnp.float32),
        in_specs=[VMEM] * 4,
        out_specs=VMEM,
        scratch_shapes=[pltpu.SemaphoreType.DMA((2,))],
        compiler_params=PARAMS,
        cost_estimate=SOON,
    )(*even, *odd)


def beside_each_other(rows, width, *tiles):
    arrays = [x for pair in tiles for x in pair]

    def kernel(*refs):
        out_ref = refs[-1]

        def run(p):
            shape = (SUBLANES, arrays[0].shape[1])
            column = lax.broadcasted_iota(jnp.int32, shape, 1)
            result = jnp.zeros(shape, jnp.float32)
            for n in range(len(tiles)):
                ref, tall = refs[2 * n + p], arrays[2 * n + p].shape[0] - SUBLANES
                moved = ref[pl.ds(tall, SUBLANES), :]
                moved = pltpu.roll(moved, n * width, 1) if n else moved
                result = jnp.where((column >= n * width) & (column < (n + 1) * width), moved, result)
            out_ref[...] = result[:out_ref.shape[0], :out_ref.shape[1]]

        by_parity(True, run)

    return pl.pallas_call(
        kernel,
        out_shape=jax.ShapeDtypeStruct((rows, len(tiles) * width), jnp.float32),
        in_specs=[VMEM] * len(arrays),
        out_specs=VMEM,
        compiler_params=PARAMS,
        cost_estimate=SOON,
    )(*arrays)


def list_pairs(p_cols, ncol, offsets):
    rows, slots = p_cols.shape
    slots_dev = slots // ncol
    nrow = lax.axis_size("row")
    heads, cap = ncol * len(offsets), rows * slots_dev

    def kernel(p_cols_ref, out_ref):
        row_at, col_at = lax.axis_index("row"), lax.axis_index("col")
        for n in range(heads):
            out_ref[n, cap] = 0

        def one_row(i, carry):
            for s in range(slots):
                half, here = s // slots_dev, s % slots_dev
                ahead = lax.rem(col_at + half, ncol)
                k = p_cols_ref[i, ahead * slots_dev + here]
                group, local = lax.div(k, rows), lax.rem(k, rows)
                steps = lax.rem(row_at + ahead - group + nrow, nrow)

                @pl.when(steps < WINDOW)
                def _():
                    head = half * len(offsets) + ahead - steps + WINDOW - 1
                    long = out_ref[head, cap]
                    out_ref[head, long] = (i * slots_dev + here) * rows + local
                    out_ref[head, cap] = long + 1

            return carry

        lax.fori_loop(0, rows, one_row, 0)

    return pl.pallas_call(
        kernel,
        out_shape=jax.ShapeDtypeStruct((heads, cap + 1), jnp.int32),
        in_specs=[SMEM],
        out_specs=SMEM,
        compiler_params=PARAMS,
        cost_estimate=SOON,
    )(p_cols)


def index_tile(source, tall, flops, *ahead):
    def kernel(source_ref, *refs):
        out_ref, sem = refs[-2:]
        copy = pltpu.make_async_copy(source_ref.at[pl.ds(tall, out_ref.shape[0])], out_ref, sem)
        copy.start()
        copy.wait()

    return pl.pallas_call(
        kernel,
        out_shape=jax.ShapeDtypeStruct((source.shape[0] - tall, source.shape[1]), jnp.float32),
        in_specs=[VMEM] * (1 + len(ahead)),
        out_specs=VMEM,
        scratch_shapes=[pltpu.SemaphoreType.DMA],
        compiler_params=PARAMS,
        cost_estimate=pl.CostEstimate(flops=flops, bytes_accessed=0, transcendentals=0),
    )(source, *ahead)


def add_products(pairs, offsets, out_cols, left, entries, total, paired):
    ncol = len(left)
    outs = out_cols.shape[1] // ncol
    block = left[0][0].shape[1]
    rows = out_cols.shape[0]
    slots_dev = out_cols.shape[1] // ncol
    cap = rows * slots_dev
    shards, indices = [], [pairs, out_cols.astype(jnp.float32)]

    def number(array, known):
        for n, x in enumerate(known):
            if x is array:
                return n
        known.append(array)
        return len(known) - 1

    left_at = [[number(x, shards) for x in part] for part in left]
    plan = [
        (offsets.index(d), p, number(cols, indices), start, [(number(x, shards), half) for x, half in pieces], lefts)
        for d, p, (cols, start), pieces, lefts in entries
    ]
    has_total = total is not None

    def kernel(*refs):
        index_refs, refs = refs[:len(indices)], refs[len(indices):]
        sums = refs[-1]
        sums[...] = refs[-2][...] if has_total else jnp.zeros_like(sums)
        col_at = lax.axis_index("col")

        def tile(n, at):
            return refs[n][pl.ds(pl.multiple_of(at * block, block), block), :]

        def run(p):
            for n, q, source, start, pieces, lefts in plan:
                if q is not None and q != p:
                    continue
                for half in lefts:
                    head = half * len(offsets) + n
                    left_shard = left_at[half][p if len(left_at[half]) > 1 else 0]

                    def one_pair(m, carry):
                        pair = index_refs[0][head, m]
                        here, local = lax.div(pair, rows), lax.rem(pair, rows)
                        i = lax.div(here, slots_dev)
                        wanted = [index_refs[1][i, col_at * outs + o] for o in range(outs)]
                        found = []
                        for shard, piece_half in pieces:
                            for t in range(slots_dev):
                                column = index_refs[source][local, start + lax.rem(col_at + piece_half, ncol) * slots_dev + t]
                                found += [(column == wanted[o], shard, t, o) for o in range(outs)]

                        @pl.when(functools.reduce(jnp.logical_or, [match for match, *_ in found]))
                        def _():
                            for match, shard, t, o in found:

                                @pl.when(match)
                                def _():
                                    sums[i, o] += product(tile(left_shard, here), tile(shard, local * slots_dev + t))

                        return carry

                    lax.fori_loop(0, index_refs[0][head, cap], one_pair, 0)

        by_parity(paired, run)

    operands = shards + ([total] if has_total else [])
    shape = (rows, outs, block, block)
    return pl.pallas_call(
        kernel,
        out_shape=jax.ShapeDtypeStruct(shape, jnp.float32),
        in_specs=[SMEM] * len(indices) + [VMEM] * len(operands),
        out_specs=VMEM,
        compiler_params=PARAMS,
        cost_estimate=SOON,
    )(*indices, *operands)


def finish(pairs, offsets, tables, wanted_at, left, rights, entries, total):
    rows, outs, block = total.shape[:3]
    nright = max(len(part) for part in rights)
    slots_dev = outs
    ncol = left.shape[0] // (rows * slots_dev * block)
    blocks = rows * slots_dev
    tall = blocks * block
    cap = blocks
    targets = rows * outs
    longest = ncol * blocks * outs * slots_dev * max(sum(len(pieces) for *_, pieces in part) for part in entries)
    shards, indices = [left], [pairs, tables]

    def number(array, known):
        for n, x in enumerate(known):
            if x is array:
                return n
        known.append(array)
        return len(known) - 1

    rights_at = [[number(x, shards) for x in part] for part in rights]
    plan = [[(offsets.index(d), start, pieces) for d, start, pieces in part] for part in entries]

    def kernel(*refs):
        brought, refs = refs[:len(indices)], refs[len(indices):]
        total_ref, out_ref, right, sums, listed, sems, index_sems = refs[len(shards):len(shards) + 7]
        index_refs = refs[len(shards) + 7:]
        index_copies = [pltpu.make_async_copy(x, y, index_sems.at[n]) for n, (x, y) in enumerate(zip(brought, index_refs))]
        for copy in index_copies:
            copy.start()
        lefts = refs[0]
        pairs_ref, tables_ref = index_refs
        col_at = lax.axis_index("col")

        def run(p):
            copies = [
                pltpu.make_async_copy(refs[n].at[pl.ds(0, tall)], right.at[pl.ds(m * tall, tall)], sems.at[m])
                for m, n in enumerate(rights_at[p])
            ]
            copies.append(pltpu.make_async_copy(total_ref, sums.at[pl.ds(0, targets)], sems.at[nright]))
            for copy in copies:
                copy.start()

            for copy in index_copies:
                copy.wait()
            long = jnp.int32(0)
            for n, start, pieces in plan[p]:
                for half in range(ncol):
                    head = half * len(offsets) + n

                    def one_pair(m, long):
                        pair = pairs_ref[head, m]
                        here, local = lax.div(pair, rows), lax.rem(pair, rows)
                        i = lax.div(here, slots_dev)
                        for shard, piece_half in pieces:
                            for t in range(slots_dev):
                                column = tables_ref[local, start + lax.rem(col_at + piece_half, ncol) * slots_dev + t]
                                code = (half * blocks + here) * nright * blocks + shard * blocks + local * slots_dev + t
                                for o in range(outs):
                                    listed[long] = code * targets + i * outs + o
                                    long += (column == tables_ref[i, wanted_at + col_at * outs + o]).astype(jnp.int32)
                        return long

                    long = lax.fori_loop(0, pairs_ref[head, cap], one_pair, long)
            for copy in copies:
                copy.wait()

            def tile(ref, at):
                return ref[pl.ds(pl.multiple_of(at * block, block), block), :]

            def some(m, carry):
                found = []
                for n in range(TOGETHER):
                    at = m * TOGETHER + n
                    code = listed[jnp.minimum(at, long - 1)]
                    tiles, target = lax.div(code, targets), lax.rem(code, targets)
                    result = product(tile(lefts, lax.div(tiles, nright * blocks)), tile(right, lax.rem(tiles, nright * blocks)))
                    found.append((jnp.where(at < long, target, targets), result))
                for target, result in found:
                    sums[target] += result
                return carry

            lax.fori_loop(0, lax.div(long + TOGETHER - 1, TOGETHER), some, 0)

        by_parity(True, run)
        copy = pltpu.make_async_copy(sums.at[pl.ds(0, targets)], out_ref, sems.at[0])
        copy.start()
        copy.wait()

    result = pl.pallas_call(
        kernel,
        out_shape=jax.ShapeDtypeStruct((targets, block, block), jnp.float32),
        in_specs=[VMEM] * (len(indices) + len(shards) + 1),
        out_specs=pl.BlockSpec(memory_space=pltpu.HBM),
        scratch_shapes=[
            pltpu.VMEM((nright * tall, block), jnp.float32),
            pltpu.VMEM((targets + 1, block, block), jnp.float32),
            pltpu.SMEM((longest + 1,), jnp.int32),
            pltpu.SemaphoreType.DMA((nright + 1,)),
            pltpu.SemaphoreType.DMA((len(indices),)),
        ]
        + [pltpu.SMEM(x.shape, x.dtype) for x in indices],
        compiler_params=PARAMS,
        cost_estimate=SOON,
    )(*indices, *shards, total.reshape(targets, block, block))
    return result.reshape(total.shape)


def on_device(p_vals, p_cols, out_cols):
    nrow, ncol = lax.axis_size("row"), lax.axis_size("col")
    rows = p_cols.shape[0]

    def permute(x, source):
        pairs = []
        for r in range(nrow):
            for c in range(ncol):
                if source(r, c) is not None:
                    from_row, from_col = source(r, c)
                    pairs.append((from_row % nrow * ncol + from_col % ncol, r * ncol + c))
        return lax.ppermute(x, ("row", "col"), pairs)

    def after(x, *others):
        return lax.optimization_barrier((x, *others))[0]

    own = p_vals.reshape(-1, p_vals.shape[-1])
    offsets = tuple(range(1 - WINDOW, ncol))
    pairs = list_pairs(p_cols, ncol, offsets)

    if ncol == 2 and nrow % 2 == 0 and rows <= SUBLANES and 9 * p_cols.shape[1] <= own.shape[1]:
        def by_core(from_even, from_odd):
            return lambda r, c: (from_odd if r % 2 else from_even)(r, c)

        def across(r, c):
            return r, c + 1

        def behind(r, c):
            return r - 2, c

        def ahead(r, c):
            return r + 2, c

        def beside(r, c):
            return r ^ 1, c

        both = (0, 1)
        tall = own.shape[0]
        first = permute(own, by_core(across, behind))
        own_cols = p_cols.astype(jnp.float32)
        mate_cols = permute(own_cols, beside)
        beside_own = permute(own, beside)
        packed = pack(own, [own_cols, mate_cols, out_cols.astype(jnp.float32)])
        second = permute(packed, by_core(behind, across))
        next_first = permute(first, lambda r, c: (r + 1, c))
        third = permute(first, lambda r, c: (r, c + 1) if r % 2 else None)
        outgoing = repack(tall, (second, second), (beside_own, packed))
        fourth = permute(outgoing, by_core(across, ahead))
        left = [[packed], [first, second]]

        back_cols = index_tile(second, tall, 0, outgoing)
        total = add_products(
            pairs,
            offsets,
            out_cols,
            left,
            [
                (0, 0, (own_cols, 0), [(packed, 0), (first, 1)], both),
                (0, 1, (own_cols, 0), [(packed, 0), (second, 1)], both),
                (1, 0, (mate_cols, 0), [(beside_own, 0)], both),
                (-1, 1, (mate_cols, 0), [(beside_own, 0)], both),
                (-2, 0, (back_cols, 0), [(second, 0)], both),
            ],
            None,
            True,
        )
        beside_other = permute(repack(tall, (first, second), (second, second), total), beside)
        beside_third = permute(third, lambda r, c: None if r % 2 else (r + 1, c))
        late_cols = index_tile(second, tall, 10**9, next_first)
        far_cols = index_tile(fourth, tall, 10**9, late_cols)
        width = 3 * p_cols.shape[1]
        own_at, mate_at, wanted_at = (n * p_cols.shape[1] for n in range(3))
        tables = beside_each_other(rows, width, (packed, packed), (late_cols, beside_other), (far_cols, far_cols))
        return finish(
            pairs,
            offsets,
            tables,
            wanted_at,
            stack(tall, (packed, first), (packed, second)),
            [[beside_other, fourth, next_first, beside_third], [beside_other, first, third, fourth, next_first]],
            [
                [
                    (1, mate_at, [(0, 1)]),
                    (-2, width + own_at, [(1, 1)]),
                    (-1, width + mate_at, [(2, 0), (3, 1)]),
                ],
                [
                    (-1, mate_at, [(0, 1)]),
                    (-2, width + mate_at, [(1, 0), (2, 1)]),
                    (1, 2 * width + mate_at, [(3, 0), (4, 1)]),
                ],
            ],
            total,
        )

    left = [[own]] + [[permute(own, lambda r, c, j=j: (r, c + j))] for j in range(1, ncol)]
    halves = tuple(range(ncol))
    own_cols = p_cols.astype(jnp.float32)
    shards, cols = {0: own}, {0: own_cols}
    for d in offsets:
        if d:
            shards[d], cols[d] = (permute(x, lambda r, c, d=d: (r + d, c)) for x in (own, own_cols))
    total = None
    for j in halves:
        sources = {d: after(x, total) if j else x for d, x in shards.items()}
        layer = {d: permute(x, lambda r, c, j=j: (r, c + j)) if j else x for d, x in sources.items()}
        entries = [(d, None, (cols[d], 0), [(x, j)], halves) for d, x in layer.items()]
        total = add_products(pairs, offsets, out_cols, left, entries, total, False)
    return total


def solution(mesh):
    placed = (P("row", "col", None, None), P("row", None), P("row", None))
    return jax.shard_map(
        on_device,
        mesh=mesh,
        in_specs=placed,
        out_specs=P("row", "col", None, None),
        check_vma=False,
    )
```

```python
import functools

import jax
import jax.numpy as jnp
from jax import lax
from jax.experimental import pallas as pl
from jax.experimental.pallas import tpu as pltpu
from jax.sharding import PartitionSpec as P

WINDOW = 3
TOGETHER = 4
SUBLANES = 8
SMEM = pl.BlockSpec(memory_space=pltpu.SMEM)
VMEM = pl.BlockSpec(memory_space=pltpu.VMEM)
PARAMS = pltpu.CompilerParams(vmem_limit_bytes=48 * 2**20)
SOON = pl.CostEstimate(flops=0, bytes_accessed=0, transcendentals=0)


def split(x):
    high = x.astype(jnp.bfloat16)
    return high, (x - high.astype(jnp.float32)).astype(jnp.bfloat16)


def product(left, right):
    left_high, left_low = split(left)
    right_high, right_low = split(right)
    return jnp.dot(
        jnp.concatenate([left_high, left_low, left_high], axis=1),
        jnp.concatenate([right_high, right_high, right_low], axis=0),
        preferred_element_type=jnp.float32,
    )


def by_parity(paired, run):
    if paired:
        parity = lax.rem(lax.axis_index("row"), 2)
        pl.when(parity == 0)(lambda: run(0))
        pl.when(parity == 1)(lambda: run(1))
    else:
        run(None)


def pack(blocks, tables, *ahead):
    tall, block = blocks.shape
    rows, slots = tables[0].shape
    tail = SUBLANES

    def kernel(*refs):
        cols_refs, blocks_ref, (out_ref, sem) = refs[:len(tables)], refs[len(tables)], refs[-2:]
        copy = pltpu.make_async_copy(blocks_ref, out_ref.at[pl.ds(0, tall)], sem)
        copy.start()
        row, column = (lax.broadcasted_iota(jnp.int32, (tail, block), d) for d in (0, 1))
        cols = jnp.zeros((tail, block), jnp.float32)
        for n, ref in enumerate(cols_refs):
            for r in range(rows):
                for s in range(slots):
                    here = (row == r) & (column == n * slots + s)
                    cols = jnp.where(here, ref[r, s], cols)
        out_ref[pl.ds(tall, tail)] = cols
        copy.wait()

    return pl.pallas_call(
        kernel,
        out_shape=jax.ShapeDtypeStruct((tall + tail, block), jnp.float32),
        in_specs=[SMEM] * len(tables) + [VMEM] * (1 + len(ahead)),
        out_specs=VMEM,
        scratch_shapes=[pltpu.SemaphoreType.DMA],
        compiler_params=PARAMS,
        cost_estimate=SOON,
    )(*tables, blocks, *ahead)


def repack(tall, even, odd, *ahead):
    def kernel(*refs):
        out_ref, sems = refs[-2:]

        def run(p):
            copies = [
                pltpu.make_async_copy(refs[2 * p].at[pl.ds(0, tall)], out_ref.at[pl.ds(0, tall)], sems.at[0]),
                pltpu.make_async_copy(refs[2 * p + 1].at[pl.ds(tall, tail)], out_ref.at[pl.ds(tall, tail)], sems.at[1]),
            ]
            for copy in copies:
                copy.start()
            for copy in copies:
                copy.wait()

        by_parity(True, run)

    tail = even[1].shape[0] - tall
    return pl.pallas_call(
        kernel,
        out_shape=jax.ShapeDtypeStruct(even[1].shape, jnp.float32),
        in_specs=[VMEM] * (4 + len(ahead)),
        out_specs=VMEM,
        scratch_shapes=[pltpu.SemaphoreType.DMA((2,))],
        compiler_params=PARAMS,
        cost_estimate=SOON,
    )(*even, *odd, *ahead)


def stack(tall, even, odd):
    def kernel(*refs):
        out_ref, sems = refs[-2:]

        def run(p):
            copies = [
                pltpu.make_async_copy(refs[2 * p + n].at[pl.ds(0, tall)], out_ref.at[pl.ds(n * tall, tall)], sems.at[n])
                for n in range(2)
            ]
            for copy in copies:
                copy.start()
            for copy in copies:
                copy.wait()

        by_parity(True, run)

    return pl.pallas_call(
        kernel,
        out_shape=jax.ShapeDtypeStruct((2 * tall, even[0].shape[1]), jnp.float32),
        in_specs=[VMEM] * 4,
        out_specs=VMEM,
        scratch_shapes=[pltpu.SemaphoreType.DMA((2,))],
        compiler_params=PARAMS,
        cost_estimate=SOON,
    )(*even, *odd)


def beside_each_other(rows, width, *tiles):
    arrays = [x for pair in tiles for x in pair]

    def kernel(*refs):
        out_ref = refs[-1]

        def run(p):
            shape = (SUBLANES, arrays[0].shape[1])
            column = lax.broadcasted_iota(jnp.int32, shape, 1)
            result = jnp.zeros(shape, jnp.float32)
            for n in range(len(tiles)):
                ref, tall = refs[2 * n + p], arrays[2 * n + p].shape[0] - SUBLANES
                moved = ref[pl.ds(tall, SUBLANES), :]
                moved = pltpu.roll(moved, n * width, 1) if n else moved
                result = jnp.where((column >= n * width) & (column < (n + 1) * width), moved, result)
            out_ref[...] = result[:out_ref.shape[0], :out_ref.shape[1]]

        by_parity(True, run)

    return pl.pallas_call(
        kernel,
        out_shape=jax.ShapeDtypeStruct((rows, len(tiles) * width), jnp.float32),
        in_specs=[VMEM] * len(arrays),
        out_specs=VMEM,
        compiler_params=PARAMS,
        cost_estimate=SOON,
    )(*arrays)


def list_pairs(p_cols, ncol, offsets):
    rows, slots = p_cols.shape
    slots_dev = slots // ncol
    nrow = lax.axis_size("row")
    heads, cap = ncol * len(offsets), rows * slots_dev

    def kernel(p_cols_ref, out_ref):
        row_at, col_at = lax.axis_index("row"), lax.axis_index("col")
        for n in range(heads):
            out_ref[n, cap] = 0

        def one_row(i, carry):
            for s in range(slots):
                half, here = s // slots_dev, s % slots_dev
                ahead = lax.rem(col_at + half, ncol)
                k = p_cols_ref[i, ahead * slots_dev + here]
                group, local = lax.div(k, rows), lax.rem(k, rows)
                steps = lax.rem(row_at + ahead - group + nrow, nrow)

                @pl.when(steps < WINDOW)
                def _():
                    head = half * len(offsets) + ahead - steps + WINDOW - 1
                    long = out_ref[head, cap]
                    out_ref[head, long] = (i * slots_dev + here) * rows + local
                    out_ref[head, cap] = long + 1

            return carry

        lax.fori_loop(0, rows, one_row, 0)

    return pl.pallas_call(
        kernel,
        out_shape=jax.ShapeDtypeStruct((heads, cap + 1), jnp.int32),
        in_specs=[SMEM],
        out_specs=SMEM,
        compiler_params=PARAMS,
        cost_estimate=SOON,
    )(p_cols)


def index_tile(source, tall, flops, *ahead):
    def kernel(source_ref, *refs):
        out_ref, sem = refs[-2:]
        copy = pltpu.make_async_copy(source_ref.at[pl.ds(tall, out_ref.shape[0])], out_ref, sem)
        copy.start()
        copy.wait()

    return pl.pallas_call(
        kernel,
        out_shape=jax.ShapeDtypeStruct((source.shape[0] - tall, source.shape[1]), jnp.float32),
        in_specs=[VMEM] * (1 + len(ahead)),
        out_specs=VMEM,
        scratch_shapes=[pltpu.SemaphoreType.DMA],
        compiler_params=PARAMS,
        cost_estimate=pl.CostEstimate(flops=flops, bytes_accessed=0, transcendentals=0),
    )(source, *ahead)


def add_products(pairs, offsets, out_cols, left, entries, total, paired):
    ncol = len(left)
    outs = out_cols.shape[1] // ncol
    block = left[0][0].shape[1]
    rows = out_cols.shape[0]
    slots_dev = out_cols.shape[1] // ncol
    cap = rows * slots_dev
    shards, indices = [], [pairs, out_cols.astype(jnp.float32)]

    def number(array, known):
        for n, x in enumerate(known):
            if x is array:
                return n
        known.append(array)
        return len(known) - 1

    left_at = [[number(x, shards) for x in part] for part in left]
    plan = [
        (offsets.index(d), p, number(cols, indices), start, [(number(x, shards), half) for x, half in pieces], lefts)
        for d, p, (cols, start), pieces, lefts in entries
    ]
    has_total = total is not None

    def kernel(*refs):
        index_refs, refs = refs[:len(indices)], refs[len(indices):]
        sums = refs[-1]
        sums[...] = refs[-2][...] if has_total else jnp.zeros_like(sums)
        col_at = lax.axis_index("col")

        def tile(n, at):
            return refs[n][pl.ds(pl.multiple_of(at * block, block), block), :]

        def run(p):
            for n, q, source, start, pieces, lefts in plan:
                if q is not None and q != p:
                    continue
                for half in lefts:
                    head = half * len(offsets) + n
                    left_shard = left_at[half][p if len(left_at[half]) > 1 else 0]

                    def one_pair(m, carry):
                        pair = index_refs[0][head, m]
                        here, local = lax.div(pair, rows), lax.rem(pair, rows)
                        i = lax.div(here, slots_dev)
                        wanted = [index_refs[1][i, col_at * outs + o] for o in range(outs)]
                        found = []
                        for shard, piece_half in pieces:
                            for t in range(slots_dev):
                                column = index_refs[source][local, start + lax.rem(col_at + piece_half, ncol) * slots_dev + t]
                                found += [(column == wanted[o], shard, t, o) for o in range(outs)]

                        @pl.when(functools.reduce(jnp.logical_or, [match for match, *_ in found]))
                        def _():
                            for match, shard, t, o in found:

                                @pl.when(match)
                                def _():
                                    sums[i, o] += product(tile(left_shard, here), tile(shard, local * slots_dev + t))

                        return carry

                    lax.fori_loop(0, index_refs[0][head, cap], one_pair, 0)

        by_parity(paired, run)

    operands = shards + ([total] if has_total else [])
    shape = (rows, outs, block, block)
    return pl.pallas_call(
        kernel,
        out_shape=jax.ShapeDtypeStruct(shape, jnp.float32),
        in_specs=[SMEM] * len(indices) + [VMEM] * len(operands),
        out_specs=VMEM,
        compiler_params=PARAMS,
        cost_estimate=SOON,
    )(*indices, *operands)


def finish(pairs, offsets, tables, wanted_at, left, rights, entries, total):
    rows, outs, block = total.shape[:3]
    nright = max(len(part) for part in rights)
    slots_dev = outs
    ncol = left.shape[0] // (rows * slots_dev * block)
    blocks = rows * slots_dev
    tall = blocks * block
    cap = blocks
    targets = rows * outs
    longest = ncol * blocks * outs * slots_dev * max(sum(len(pieces) for *_, pieces in part) for part in entries)
    shards, indices = [left], [pairs, tables]

    def number(array, known):
        for n, x in enumerate(known):
            if x is array:
                return n
        known.append(array)
        return len(known) - 1

    rights_at = [[number(x, shards) for x in part] for part in rights]
    plan = [[(offsets.index(d), start, pieces) for d, start, pieces in part] for part in entries]

    def kernel(*refs):
        brought, refs = refs[:len(indices)], refs[len(indices):]
        total_ref, out_ref, right, sums, listed, sems, index_sems = refs[len(shards):len(shards) + 7]
        index_refs = refs[len(shards) + 7:]
        index_copies = [pltpu.make_async_copy(x, y, index_sems.at[n]) for n, (x, y) in enumerate(zip(brought, index_refs))]
        for copy in index_copies:
            copy.start()
        lefts = refs[0]
        pairs_ref, tables_ref = index_refs
        col_at = lax.axis_index("col")

        def run(p):
            copies = [
                pltpu.make_async_copy(refs[n].at[pl.ds(0, tall)], right.at[pl.ds(m * tall, tall)], sems.at[m])
                for m, n in enumerate(rights_at[p])
            ]
            copies.append(pltpu.make_async_copy(total_ref, sums.at[pl.ds(0, targets)], sems.at[nright]))
            for copy in copies:
                copy.start()

            for copy in index_copies:
                copy.wait()
            long = jnp.int32(0)
            for n, start, pieces in plan[p]:
                for half in range(ncol):
                    head = half * len(offsets) + n

                    def one_pair(m, long):
                        pair = pairs_ref[head, m]
                        here, local = lax.div(pair, rows), lax.rem(pair, rows)
                        i = lax.div(here, slots_dev)
                        for shard, piece_half in pieces:
                            for t in range(slots_dev):
                                column = tables_ref[local, start + lax.rem(col_at + piece_half, ncol) * slots_dev + t]
                                code = (half * blocks + here) * nright * blocks + shard * blocks + local * slots_dev + t
                                for o in range(outs):
                                    listed[long] = code * targets + i * outs + o
                                    long += (column == tables_ref[i, wanted_at + col_at * outs + o]).astype(jnp.int32)
                        return long

                    long = lax.fori_loop(0, pairs_ref[head, cap], one_pair, long)
            for copy in copies:
                copy.wait()

            def tile(ref, at):
                return ref[pl.ds(pl.multiple_of(at * block, block), block), :]

            def some(m, carry):
                found = []
                for n in range(TOGETHER):
                    at = m * TOGETHER + n
                    code = listed[jnp.minimum(at, long - 1)]
                    tiles, target = lax.div(code, targets), lax.rem(code, targets)
                    result = product(tile(lefts, lax.div(tiles, nright * blocks)), tile(right, lax.rem(tiles, nright * blocks)))
                    found.append((jnp.where(at < long, target, targets), result))
                for target, result in found:
                    sums[target] += result
                return carry

            lax.fori_loop(0, lax.div(long + TOGETHER - 1, TOGETHER), some, 0)

        by_parity(True, run)
        copy = pltpu.make_async_copy(sums.at[pl.ds(0, targets)], out_ref, sems.at[0])
        copy.start()
        copy.wait()

    result = pl.pallas_call(
        kernel,
        out_shape=jax.ShapeDtypeStruct((targets, block, block), jnp.float32),
        in_specs=[VMEM] * (len(indices) + len(shards) + 1),
        out_specs=pl.BlockSpec(memory_space=pltpu.HBM),
        scratch_shapes=[
            pltpu.VMEM((nright * tall, block), jnp.float32),
            pltpu.VMEM((targets + 1, block, block), jnp.float32),
            pltpu.SMEM((longest + 1,), jnp.int32),
            pltpu.SemaphoreType.DMA((nright + 1,)),
            pltpu.SemaphoreType.DMA((len(indices),)),
        ]
        + [pltpu.SMEM(x.shape, x.dtype) for x in indices],
        compiler_params=PARAMS,
        cost_estimate=SOON,
    )(*indices, *shards, total.reshape(targets, block, block))
    return result.reshape(total.shape)


def on_device(p_vals, p_cols, out_cols):
    nrow, ncol = lax.axis_size("row"), lax.axis_size("col")
    rows = p_cols.shape[0]

    def permute(x, source):
        pairs = []
        for r in range(nrow):
            for c in range(ncol):
                if source(r, c) is not None:
                    from_row, from_col = source(r, c)
                    pairs.append((from_row % nrow * ncol + from_col % ncol, r * ncol + c))
        return lax.ppermute(x, ("row", "col"), pairs)

    def after(x, *others):
        return lax.optimization_barrier((x, *others))[0]

    own = p_vals.reshape(-1, p_vals.shape[-1])
    offsets = tuple(range(1 - WINDOW, ncol))
    pairs = list_pairs(p_cols, ncol, offsets)

    if ncol == 2 and nrow % 2 == 0 and rows <= SUBLANES and 9 * p_cols.shape[1] <= own.shape[1]:
        def by_core(from_even, from_odd):
            return lambda r, c: (from_odd if r % 2 else from_even)(r, c)

        def across(r, c):
            return r, c + 1

        def behind(r, c):
            return r - 2, c

        def ahead(r, c):
            return r + 2, c

        def beside(r, c):
            return r ^ 1, c

        both = (0, 1)
        tall = own.shape[0]
        first = permute(own, by_core(across, behind))
        own_cols = p_cols.astype(jnp.float32)
        mate_cols = permute(own_cols, beside)
        beside_own = permute(own, beside)
        packed = pack(own, [own_cols, mate_cols, out_cols.astype(jnp.float32)], pairs)
        second = permute(packed, by_core(behind, across))
        next_first = permute(first, lambda r, c: (r + 1, c))
        third = permute(first, lambda r, c: (r, c + 1) if r % 2 else None)
        outgoing = repack(tall, (second, second), (beside_own, packed))
        fourth = permute(outgoing, by_core(across, ahead))
        left = [[packed], [first, second]]

        beside_other = permute(repack(tall, (first, second), (second, second)), beside)
        back_cols = index_tile(second, tall, 0, outgoing)
        width = 3 * p_cols.shape[1]
        own_at, mate_at, wanted_at = (n * p_cols.shape[1] for n in range(3))

        def add(entries, total):
            return add_products(pairs, offsets, out_cols, left, entries, total, True)

        total = add(
            [
                (0, 0, (own_cols, 0), [(packed, 0), (first, 1)], both),
                (0, 1, (own_cols, 0), [(packed, 0), (second, 1)], both),
                (1, 0, (mate_cols, 0), [(beside_own, 0)], both),
                (-1, 1, (mate_cols, 0), [(beside_own, 0)], both),
                (-2, 0, (back_cols, own_at), [(second, 0)], both),
            ],
            None,
        )
        passed_on = repack(tall, (third, packed), (third, packed), total)
        beside_third = permute(passed_on, lambda r, c: None if r % 2 else (r + 1, c))
        mate_back_cols = index_tile(beside_other, tall, 0)
        total = add(
            [
                (1, 0, (mate_cols, 0), [(beside_other, 1)], both),
                (-1, 1, (mate_cols, 0), [(beside_other, 1)], both),
                (-2, 1, (mate_back_cols, mate_at), [(first, 0)], both),
            ],
            total,
        )
        late_cols = index_tile(second, tall, 10**9, next_first)
        far_cols = index_tile(fourth, tall, 10**9, late_cols, total)
        tables = beside_each_other(rows, width, (packed, packed), (late_cols, beside_other), (far_cols, far_cols))
        return finish(
            pairs,
            offsets,
            tables,
            wanted_at,
            stack(tall, (packed, first), (packed, second)),
            [[fourth, next_first, beside_third], [third, fourth, next_first]],
            [
                [
                    (-2, width + own_at, [(0, 1)]),
                    (-1, width + mate_at, [(1, 0), (2, 1)]),
                ],
                [
                    (-2, width + mate_at, [(0, 1)]),
                    (1, 2 * width + mate_at, [(1, 0), (2, 1)]),
                ],
            ],
            total,
        )

    left = [[own]] + [[permute(own, lambda r, c, j=j: (r, c + j))] for j in range(1, ncol)]
    halves = tuple(range(ncol))
    own_cols = p_cols.astype(jnp.float32)
    shards, cols = {0: own}, {0: own_cols}
    for d in offsets:
        if d:
            shards[d], cols[d] = (permute(x, lambda r, c, d=d: (r + d, c)) for x in (own, own_cols))
    total = None
    for j in halves:
        sources = {d: after(x, total) if j else x for d, x in shards.items()}
        layer = {d: permute(x, lambda r, c, j=j: (r, c + j)) if j else x for d, x in sources.items()}
        entries = [(d, None, (cols[d], 0), [(x, j)], halves) for d, x in layer.items()]
        total = add_products(pairs, offsets, out_cols, left, entries, total, False)
    return total


def solution(mesh):
    placed = (P("row", "col", None, None), P("row", None), P("row", None))
    return jax.shard_map(
        on_device,
        mesh=mesh,
        in_specs=placed,
        out_specs=P("row", "col", None, None),
        check_vma=False,
    )
```

```python
import functools

import jax
import jax.numpy as jnp
from jax import lax
from jax.experimental import pallas as pl
from jax.experimental.pallas import tpu as pltpu
from jax.sharding import PartitionSpec as P

WINDOW = 3
TOGETHER = 4
SUBLANES = 8
SMEM = pl.BlockSpec(memory_space=pltpu.SMEM)
VMEM = pl.BlockSpec(memory_space=pltpu.VMEM)
PARAMS = pltpu.CompilerParams(vmem_limit_bytes=48 * 2**20)
SOON = pl.CostEstimate(flops=0, bytes_accessed=0, transcendentals=0)


def split(x):
    high = x.astype(jnp.bfloat16)
    return high, (x - high.astype(jnp.float32)).astype(jnp.bfloat16)


def product(left, right):
    left_high, left_low = split(left)
    right_high, right_low = split(right)
    return jnp.dot(
        jnp.concatenate([left_high, left_low, left_high], axis=1),
        jnp.concatenate([right_high, right_high, right_low], axis=0),
        preferred_element_type=jnp.float32,
    )


def by_parity(paired, run):
    if paired:
        parity = lax.rem(lax.axis_index("row"), 2)
        pl.when(parity == 0)(lambda: run(0))
        pl.when(parity == 1)(lambda: run(1))
    else:
        run(None)


def pack(blocks, tables, *ahead):
    tall, block = blocks.shape
    rows, slots = tables[0].shape
    tail = SUBLANES

    def kernel(*refs):
        cols_refs, blocks_ref, (out_ref, sem) = refs[:len(tables)], refs[len(tables)], refs[-2:]
        copy = pltpu.make_async_copy(blocks_ref, out_ref.at[pl.ds(0, tall)], sem)
        copy.start()
        row, column = (lax.broadcasted_iota(jnp.int32, (tail, block), d) for d in (0, 1))
        cols = jnp.zeros((tail, block), jnp.float32)
        for n, ref in enumerate(cols_refs):
            for r in range(rows):
                for s in range(slots):
                    here = (row == r) & (column == n * slots + s)
                    cols = jnp.where(here, ref[r, s], cols)
        out_ref[pl.ds(tall, tail)] = cols
        copy.wait()

    return pl.pallas_call(
        kernel,
        out_shape=jax.ShapeDtypeStruct((tall + tail, block), jnp.float32),
        in_specs=[SMEM] * len(tables) + [VMEM] * (1 + len(ahead)),
        out_specs=VMEM,
        scratch_shapes=[pltpu.SemaphoreType.DMA],
        compiler_params=PARAMS,
        cost_estimate=SOON,
    )(*tables, blocks, *ahead)


def repack(tall, even, odd, *ahead):
    def kernel(*refs):
        out_ref, sems = refs[-2:]

        def run(p):
            copies = [
                pltpu.make_async_copy(refs[2 * p].at[pl.ds(0, tall)], out_ref.at[pl.ds(0, tall)], sems.at[0]),
                pltpu.make_async_copy(refs[2 * p + 1].at[pl.ds(tall, tail)], out_ref.at[pl.ds(tall, tail)], sems.at[1]),
            ]
            for copy in copies:
                copy.start()
            for copy in copies:
                copy.wait()

        by_parity(True, run)

    tail = even[1].shape[0] - tall
    return pl.pallas_call(
        kernel,
        out_shape=jax.ShapeDtypeStruct(even[1].shape, jnp.float32),
        in_specs=[VMEM] * (4 + len(ahead)),
        out_specs=VMEM,
        scratch_shapes=[pltpu.SemaphoreType.DMA((2,))],
        compiler_params=PARAMS,
        cost_estimate=SOON,
    )(*even, *odd, *ahead)


def stack(tall, even, odd):
    def kernel(*refs):
        out_ref, sems = refs[-2:]

        def run(p):
            copies = [
                pltpu.make_async_copy(refs[2 * p + n].at[pl.ds(0, tall)], out_ref.at[pl.ds(n * tall, tall)], sems.at[n])
                for n in range(2)
            ]
            for copy in copies:
                copy.start()
            for copy in copies:
                copy.wait()

        by_parity(True, run)

    return pl.pallas_call(
        kernel,
        out_shape=jax.ShapeDtypeStruct((2 * tall, even[0].shape[1]), jnp.float32),
        in_specs=[VMEM] * 4,
        out_specs=VMEM,
        scratch_shapes=[pltpu.SemaphoreType.DMA((2,))],
        compiler_params=PARAMS,
        cost_estimate=SOON,
    )(*even, *odd)


def beside_each_other(rows, width, *tiles):
    arrays = [x for pair in tiles for x in pair]

    def kernel(*refs):
        out_ref = refs[-1]

        def run(p):
            shape = (SUBLANES, arrays[0].shape[1])
            column = lax.broadcasted_iota(jnp.int32, shape, 1)
            result = jnp.zeros(shape, jnp.float32)
            for n in range(len(tiles)):
                ref, tall = refs[2 * n + p], arrays[2 * n + p].shape[0] - SUBLANES
                moved = ref[pl.ds(tall, SUBLANES), :]
                moved = pltpu.roll(moved, n * width, 1) if n else moved
                result = jnp.where((column >= n * width) & (column < (n + 1) * width), moved, result)
            out_ref[...] = result[:out_ref.shape[0], :out_ref.shape[1]]

        by_parity(True, run)

    return pl.pallas_call(
        kernel,
        out_shape=jax.ShapeDtypeStruct((rows, len(tiles) * width), jnp.float32),
        in_specs=[VMEM] * len(arrays),
        out_specs=VMEM,
        compiler_params=PARAMS,
        cost_estimate=SOON,
    )(*arrays)


def list_pairs(p_cols, ncol, offsets):
    rows, slots = p_cols.shape
    slots_dev = slots // ncol
    nrow = lax.axis_size("row")
    heads, cap = ncol * len(offsets), rows * slots_dev

    def kernel(p_cols_ref, out_ref):
        row_at, col_at = lax.axis_index("row"), lax.axis_index("col")
        for n in range(heads):
            out_ref[n, cap] = 0

        def one_row(i, carry):
            for s in range(slots):
                half, here = s // slots_dev, s % slots_dev
                ahead = lax.rem(col_at + half, ncol)
                k = p_cols_ref[i, ahead * slots_dev + here]
                group, local = lax.div(k, rows), lax.rem(k, rows)
                steps = lax.rem(row_at + ahead - group + nrow, nrow)

                @pl.when(steps < WINDOW)
                def _():
                    head = half * len(offsets) + ahead - steps + WINDOW - 1
                    long = out_ref[head, cap]
                    out_ref[head, long] = (i * slots_dev + here) * rows + local
                    out_ref[head, cap] = long + 1

            return carry

        lax.fori_loop(0, rows, one_row, 0)

    return pl.pallas_call(
        kernel,
        out_shape=jax.ShapeDtypeStruct((heads, cap + 1), jnp.int32),
        in_specs=[SMEM],
        out_specs=SMEM,
        compiler_params=PARAMS,
        cost_estimate=SOON,
    )(p_cols)


def index_tile(source, tall, flops, *ahead):
    def kernel(source_ref, *refs):
        out_ref, sem = refs[-2:]
        copy = pltpu.make_async_copy(source_ref.at[pl.ds(tall, out_ref.shape[0])], out_ref, sem)
        copy.start()
        copy.wait()

    return pl.pallas_call(
        kernel,
        out_shape=jax.ShapeDtypeStruct((source.shape[0] - tall, source.shape[1]), jnp.float32),
        in_specs=[VMEM] * (1 + len(ahead)),
        out_specs=VMEM,
        scratch_shapes=[pltpu.SemaphoreType.DMA],
        compiler_params=PARAMS,
        cost_estimate=pl.CostEstimate(flops=flops, bytes_accessed=0, transcendentals=0),
    )(source, *ahead)


def add_products(pairs, offsets, out_cols, left, entries, total, paired):
    ncol = len(left)
    outs = out_cols.shape[1] // ncol
    block = left[0][0].shape[1]
    rows = out_cols.shape[0]
    slots_dev = out_cols.shape[1] // ncol
    cap = rows * slots_dev
    shards, indices = [], [pairs, out_cols.astype(jnp.float32)]

    def number(array, known):
        for n, x in enumerate(known):
            if x is array:
                return n
        known.append(array)
        return len(known) - 1

    left_at = [[number(x, shards) for x in part] for part in left]
    plan = [
        (offsets.index(d), p, number(cols, indices), start, [(number(x, shards), half) for x, half in pieces], lefts)
        for d, p, (cols, start), pieces, lefts in entries
    ]
    has_total = total is not None

    def kernel(*refs):
        index_refs, refs = refs[:len(indices)], refs[len(indices):]
        sums = refs[-1]
        sums[...] = refs[-2][...] if has_total else jnp.zeros_like(sums)
        col_at = lax.axis_index("col")

        def tile(n, at):
            return refs[n][pl.ds(pl.multiple_of(at * block, block), block), :]

        def run(p):
            for n, q, source, start, pieces, lefts in plan:
                if q is not None and q != p:
                    continue
                for half in lefts:
                    head = half * len(offsets) + n
                    left_shard = left_at[half][p if len(left_at[half]) > 1 else 0]

                    def one_pair(m, carry):
                        pair = index_refs[0][head, m]
                        here, local = lax.div(pair, rows), lax.rem(pair, rows)
                        i = lax.div(here, slots_dev)
                        wanted = [index_refs[1][i, col_at * outs + o] for o in range(outs)]
                        found = []
                        for shard, piece_half in pieces:
                            for t in range(slots_dev):
                                column = index_refs[source][local, start + lax.rem(col_at + piece_half, ncol) * slots_dev + t]
                                found += [(column == wanted[o], shard, t, o) for o in range(outs)]

                        @pl.when(functools.reduce(jnp.logical_or, [match for match, *_ in found]))
                        def _():
                            for match, shard, t, o in found:

                                @pl.when(match)
                                def _():
                                    sums[i, o] += product(tile(left_shard, here), tile(shard, local * slots_dev + t))

                        return carry

                    lax.fori_loop(0, index_refs[0][head, cap], one_pair, 0)

        by_parity(paired, run)

    operands = shards + ([total] if has_total else [])
    shape = (rows, outs, block, block)
    return pl.pallas_call(
        kernel,
        out_shape=jax.ShapeDtypeStruct(shape, jnp.float32),
        in_specs=[SMEM] * len(indices) + [VMEM] * len(operands),
        out_specs=VMEM,
        compiler_params=PARAMS,
        cost_estimate=SOON,
    )(*indices, *operands)


def finish(pairs, offsets, tables, wanted_at, left, rights, entries, total):
    rows, outs, block = total.shape[:3]
    nright = max(len(part) for part in rights)
    slots_dev = outs
    ncol = left.shape[0] // (rows * slots_dev * block)
    blocks = rows * slots_dev
    tall = blocks * block
    cap = blocks
    targets = rows * outs
    longest = ncol * blocks * outs * slots_dev * max(sum(len(pieces) for *_, pieces in part) for part in entries)
    shards, indices = [left], [pairs, tables]

    def number(array, known):
        for n, x in enumerate(known):
            if x is array:
                return n
        known.append(array)
        return len(known) - 1

    rights_at = [[number(x, shards) for x in part] for part in rights]
    plan = [[(offsets.index(d), start, pieces) for d, start, pieces in part] for part in entries]

    def kernel(*refs):
        brought, refs = refs[:len(indices)], refs[len(indices):]
        total_ref, out_ref, right, sums, listed, sems, index_sems = refs[len(shards):len(shards) + 7]
        index_refs = refs[len(shards) + 7:]
        index_copies = [pltpu.make_async_copy(x, y, index_sems.at[n]) for n, (x, y) in enumerate(zip(brought, index_refs))]
        for copy in index_copies:
            copy.start()
        lefts = refs[0]
        pairs_ref, tables_ref = index_refs
        col_at = lax.axis_index("col")

        def run(p):
            copies = [
                pltpu.make_async_copy(refs[n].at[pl.ds(0, tall)], right.at[pl.ds(m * tall, tall)], sems.at[m])
                for m, n in enumerate(rights_at[p])
            ]
            copies.append(pltpu.make_async_copy(total_ref, sums.at[pl.ds(0, targets)], sems.at[nright]))
            for copy in copies:
                copy.start()

            for copy in index_copies:
                copy.wait()
            long = jnp.int32(0)
            for n, start, pieces in plan[p]:
                for half in range(ncol):
                    head = half * len(offsets) + n

                    def one_pair(m, long):
                        pair = pairs_ref[head, m]
                        here, local = lax.div(pair, rows), lax.rem(pair, rows)
                        i = lax.div(here, slots_dev)
                        for shard, piece_half in pieces:
                            for t in range(slots_dev):
                                column = tables_ref[local, start + lax.rem(col_at + piece_half, ncol) * slots_dev + t]
                                code = (half * blocks + here) * nright * blocks + shard * blocks + local * slots_dev + t
                                for o in range(outs):
                                    listed[long] = code * targets + i * outs + o
                                    long += (column == tables_ref[i, wanted_at + col_at * outs + o]).astype(jnp.int32)
                        return long

                    long = lax.fori_loop(0, pairs_ref[head, cap], one_pair, long)
            for copy in copies:
                copy.wait()

            def tile(ref, at):
                return ref[pl.ds(pl.multiple_of(at * block, block), block), :]

            def some(m, carry):
                found = []
                for n in range(TOGETHER):
                    at = m * TOGETHER + n
                    code = listed[jnp.minimum(at, long - 1)]
                    tiles, target = lax.div(code, targets), lax.rem(code, targets)
                    result = product(tile(lefts, lax.div(tiles, nright * blocks)), tile(right, lax.rem(tiles, nright * blocks)))
                    found.append((jnp.where(at < long, target, targets), result))
                for target, result in found:
                    sums[target] += result
                return carry

            lax.fori_loop(0, lax.div(long + TOGETHER - 1, TOGETHER), some, 0)

        by_parity(True, run)
        copy = pltpu.make_async_copy(sums.at[pl.ds(0, targets)], out_ref, sems.at[0])
        copy.start()
        copy.wait()

    result = pl.pallas_call(
        kernel,
        out_shape=jax.ShapeDtypeStruct((targets, block, block), jnp.float32),
        in_specs=[VMEM] * (len(indices) + len(shards) + 1),
        out_specs=pl.BlockSpec(memory_space=pltpu.HBM),
        scratch_shapes=[
            pltpu.VMEM((nright * tall, block), jnp.float32),
            pltpu.VMEM((targets + 1, block, block), jnp.float32),
            pltpu.SMEM((longest + 1,), jnp.int32),
            pltpu.SemaphoreType.DMA((nright + 1,)),
            pltpu.SemaphoreType.DMA((len(indices),)),
        ]
        + [pltpu.SMEM(x.shape, x.dtype) for x in indices],
        compiler_params=PARAMS,
        cost_estimate=SOON,
    )(*indices, *shards, total.reshape(targets, block, block))
    return result.reshape(total.shape)


def on_device(p_vals, p_cols, out_cols):
    nrow, ncol = lax.axis_size("row"), lax.axis_size("col")
    rows = p_cols.shape[0]

    def permute(x, source):
        pairs = []
        for r in range(nrow):
            for c in range(ncol):
                if source(r, c) is not None:
                    from_row, from_col = source(r, c)
                    pairs.append((from_row % nrow * ncol + from_col % ncol, r * ncol + c))
        return lax.ppermute(x, ("row", "col"), pairs)

    def after(x, *others):
        return lax.optimization_barrier((x, *others))[0]

    own = p_vals.reshape(-1, p_vals.shape[-1])
    offsets = tuple(range(1 - WINDOW, ncol))
    pairs = list_pairs(p_cols, ncol, offsets)

    if ncol == 2 and nrow % 2 == 0 and rows <= SUBLANES and 9 * p_cols.shape[1] <= own.shape[1]:
        def by_core(from_even, from_odd):
            return lambda r, c: (from_odd if r % 2 else from_even)(r, c)

        def across(r, c):
            return r, c + 1

        def behind(r, c):
            return r - 2, c

        def ahead(r, c):
            return r + 2, c

        def beside(r, c):
            return r ^ 1, c

        both = (0, 1)
        tall = own.shape[0]
        first = permute(own, by_core(across, behind))
        own_cols = p_cols.astype(jnp.float32)
        mate_cols = permute(own_cols, beside)
        beside_own = permute(own, beside)
        packed = pack(own, [own_cols, mate_cols, out_cols.astype(jnp.float32)], pairs)
        second = permute(packed, by_core(behind, across))
        next_first = permute(first, lambda r, c: (r + 1, c))
        third = permute(first, lambda r, c: (r, c + 1) if r % 2 else None)
        outgoing = repack(tall, (second, second), (beside_own, packed))
        fourth = permute(outgoing, by_core(across, ahead))
        left = [[packed], [first, second]]

        beside_other = permute(repack(tall, (first, second), (second, second)), beside)
        back_cols = index_tile(second, tall, 0, outgoing)
        width = 3 * p_cols.shape[1]
        own_at, mate_at, wanted_at = (n * p_cols.shape[1] for n in range(3))

        def add(entries, total):
            return add_products(pairs, offsets, out_cols, left, entries, total, True)

        total = add(
            [
                (0, 0, (own_cols, 0), [(packed, 0), (first, 1)], both),
                (0, 1, (own_cols, 0), [(packed, 0), (second, 1)], both),
                (1, 0, (mate_cols, 0), [(beside_own, 0)], both),
                (-1, 1, (mate_cols, 0), [(beside_own, 0)], both),
                (-2, 0, (back_cols, own_at), [(second, 0)], both),
            ],
            None,
        )
        passed_on = repack(tall, (third, packed), (third, packed), total)
        beside_third = permute(passed_on, lambda r, c: None if r % 2 else (r + 1, c))
        mate_back_cols = index_tile(beside_other, tall, 0)
        total = add(
            [
                (1, 0, (mate_cols, 0), [(beside_other, 1)], both),
                (-1, 1, (mate_cols, 0), [(beside_other, 1)], both),
                (-2, 1, (mate_back_cols, mate_at), [(first, 0), (third, 1)], both),
                (-1, 0, (back_cols, mate_at), [(next_first, 0)], both),
            ],
            total,
        )
        late_cols = index_tile(second, tall, 10**9, next_first)
        far_cols = index_tile(fourth, tall, 10**9, late_cols, total)
        tables = beside_each_other(rows, width, (packed, packed), (late_cols, beside_other), (far_cols, far_cols))
        return finish(
            pairs,
            offsets,
            tables,
            wanted_at,
            stack(tall, (packed, first), (packed, second)),
            [[fourth, beside_third], [fourth, next_first]],
            [
                [
                    (-2, width + own_at, [(0, 1)]),
                    (-1, width + mate_at, [(1, 1)]),
                ],
                [
                    (1, 2 * width + mate_at, [(0, 0), (1, 1)]),
                ],
            ],
            total,
        )

    left = [[own]] + [[permute(own, lambda r, c, j=j: (r, c + j))] for j in range(1, ncol)]
    halves = tuple(range(ncol))
    own_cols = p_cols.astype(jnp.float32)
    shards, cols = {0: own}, {0: own_cols}
    for d in offsets:
        if d:
            shards[d], cols[d] = (permute(x, lambda r, c, d=d: (r + d, c)) for x in (own, own_cols))
    total = None
    for j in halves:
        sources = {d: after(x, total) if j else x for d, x in shards.items()}
        layer = {d: permute(x, lambda r, c, j=j: (r, c + j)) if j else x for d, x in sources.items()}
        entries = [(d, None, (cols[d], 0), [(x, j)], halves) for d, x in layer.items()]
        total = add_products(pairs, offsets, out_cols, left, entries, total, False)
    return total


def solution(mesh):
    placed = (P("row", "col", None, None), P("row", None), P("row", None))
    return jax.shard_map(
        on_device,
        mesh=mesh,
        in_specs=placed,
        out_specs=P("row", "col", None, None),
        check_vma=False,
    )
```

```python
import functools

import jax
import jax.numpy as jnp
from jax import lax
from jax.experimental import pallas as pl
from jax.experimental.pallas import tpu as pltpu
from jax.sharding import PartitionSpec as P

WINDOW = 3
TOGETHER = 4
SUBLANES = 8
SMEM = pl.BlockSpec(memory_space=pltpu.SMEM)
VMEM = pl.BlockSpec(memory_space=pltpu.VMEM)
PARAMS = pltpu.CompilerParams(vmem_limit_bytes=48 * 2**20)
SOON = pl.CostEstimate(flops=0, bytes_accessed=0, transcendentals=0)


def split(x):
    high = x.astype(jnp.bfloat16)
    return high, (x - high.astype(jnp.float32)).astype(jnp.bfloat16)


def product(left, right):
    left_high, left_low = split(left)
    right_high, right_low = split(right)
    return jnp.dot(
        jnp.concatenate([left_high, left_low, left_high], axis=1),
        jnp.concatenate([right_high, right_high, right_low], axis=0),
        preferred_element_type=jnp.float32,
    )


def by_parity(paired, run):
    if paired:
        parity = lax.rem(lax.axis_index("row"), 2)
        pl.when(parity == 0)(lambda: run(0))
        pl.when(parity == 1)(lambda: run(1))
    else:
        run(None)


def pack(blocks, tables, *ahead):
    tall, block = blocks.shape
    rows, slots = tables[0].shape
    tail = SUBLANES

    def kernel(*refs):
        cols_refs, blocks_ref, (out_ref, sem) = refs[:len(tables)], refs[len(tables)], refs[-2:]
        copy = pltpu.make_async_copy(blocks_ref, out_ref.at[pl.ds(0, tall)], sem)
        copy.start()
        row, column = (lax.broadcasted_iota(jnp.int32, (tail, block), d) for d in (0, 1))
        cols = jnp.zeros((tail, block), jnp.float32)
        for n, ref in enumerate(cols_refs):
            for r in range(rows):
                for s in range(slots):
                    here = (row == r) & (column == n * slots + s)
                    cols = jnp.where(here, ref[r, s], cols)
        out_ref[pl.ds(tall, tail)] = cols
        copy.wait()

    return pl.pallas_call(
        kernel,
        out_shape=jax.ShapeDtypeStruct((tall + tail, block), jnp.float32),
        in_specs=[SMEM] * len(tables) + [VMEM] * (1 + len(ahead)),
        out_specs=VMEM,
        scratch_shapes=[pltpu.SemaphoreType.DMA],
        compiler_params=PARAMS,
        cost_estimate=SOON,
    )(*tables, blocks, *ahead)


def repack(tall, even, odd, *ahead):
    def kernel(*refs):
        out_ref, sems = refs[-2:]

        def run(p):
            copies = [
                pltpu.make_async_copy(refs[2 * p].at[pl.ds(0, tall)], out_ref.at[pl.ds(0, tall)], sems.at[0]),
                pltpu.make_async_copy(refs[2 * p + 1].at[pl.ds(tall, tail)], out_ref.at[pl.ds(tall, tail)], sems.at[1]),
            ]
            for copy in copies:
                copy.start()
            for copy in copies:
                copy.wait()

        by_parity(True, run)

    tail = even[1].shape[0] - tall
    return pl.pallas_call(
        kernel,
        out_shape=jax.ShapeDtypeStruct(even[1].shape, jnp.float32),
        in_specs=[VMEM] * (4 + len(ahead)),
        out_specs=VMEM,
        scratch_shapes=[pltpu.SemaphoreType.DMA((2,))],
        compiler_params=PARAMS,
        cost_estimate=SOON,
    )(*even, *odd, *ahead)


def stack(tall, even, odd):
    def kernel(*refs):
        out_ref, sems = refs[-2:]

        def run(p):
            copies = [
                pltpu.make_async_copy(refs[2 * p + n].at[pl.ds(0, tall)], out_ref.at[pl.ds(n * tall, tall)], sems.at[n])
                for n in range(2)
            ]
            for copy in copies:
                copy.start()
            for copy in copies:
                copy.wait()

        by_parity(True, run)

    return pl.pallas_call(
        kernel,
        out_shape=jax.ShapeDtypeStruct((2 * tall, even[0].shape[1]), jnp.float32),
        in_specs=[VMEM] * 4,
        out_specs=VMEM,
        scratch_shapes=[pltpu.SemaphoreType.DMA((2,))],
        compiler_params=PARAMS,
        cost_estimate=SOON,
    )(*even, *odd)


def beside_each_other(rows, width, *tiles):
    arrays = [x for pair in tiles for x in pair]

    def kernel(*refs):
        out_ref = refs[-1]

        def run(p):
            shape = (SUBLANES, arrays[0].shape[1])
            column = lax.broadcasted_iota(jnp.int32, shape, 1)
            result = jnp.zeros(shape, jnp.float32)
            for n in range(len(tiles)):
                ref, tall = refs[2 * n + p], arrays[2 * n + p].shape[0] - SUBLANES
                moved = ref[pl.ds(tall, SUBLANES), :]
                moved = pltpu.roll(moved, n * width, 1) if n else moved
                result = jnp.where((column >= n * width) & (column < (n + 1) * width), moved, result)
            out_ref[...] = result[:out_ref.shape[0], :out_ref.shape[1]]

        by_parity(True, run)

    return pl.pallas_call(
        kernel,
        out_shape=jax.ShapeDtypeStruct((rows, len(tiles) * width), jnp.float32),
        in_specs=[VMEM] * len(arrays),
        out_specs=VMEM,
        compiler_params=PARAMS,
        cost_estimate=SOON,
    )(*arrays)


def list_pairs(p_cols, ncol, offsets):
    rows, slots = p_cols.shape
    slots_dev = slots // ncol
    nrow = lax.axis_size("row")
    heads, cap = ncol * len(offsets), rows * slots_dev

    def kernel(p_cols_ref, out_ref):
        row_at, col_at = lax.axis_index("row"), lax.axis_index("col")
        for n in range(heads):
            out_ref[n, cap] = 0

        def one_row(i, carry):
            for s in range(slots):
                half, here = s // slots_dev, s % slots_dev
                ahead = lax.rem(col_at + half, ncol)
                k = p_cols_ref[i, ahead * slots_dev + here]
                group, local = lax.div(k, rows), lax.rem(k, rows)
                steps = lax.rem(row_at + ahead - group + nrow, nrow)

                @pl.when(steps < WINDOW)
                def _():
                    head = half * len(offsets) + ahead - steps + WINDOW - 1
                    long = out_ref[head, cap]
                    out_ref[head, long] = (i * slots_dev + here) * rows + local
                    out_ref[head, cap] = long + 1

            return carry

        lax.fori_loop(0, rows, one_row, 0)

    return pl.pallas_call(
        kernel,
        out_shape=jax.ShapeDtypeStruct((heads, cap + 1), jnp.int32),
        in_specs=[SMEM],
        out_specs=SMEM,
        compiler_params=PARAMS,
        cost_estimate=SOON,
    )(p_cols)


def index_tile(source, tall, flops, *ahead):
    def kernel(source_ref, *refs):
        out_ref, sem = refs[-2:]
        copy = pltpu.make_async_copy(source_ref.at[pl.ds(tall, out_ref.shape[0])], out_ref, sem)
        copy.start()
        copy.wait()

    return pl.pallas_call(
        kernel,
        out_shape=jax.ShapeDtypeStruct((source.shape[0] - tall, source.shape[1]), jnp.float32),
        in_specs=[VMEM] * (1 + len(ahead)),
        out_specs=VMEM,
        scratch_shapes=[pltpu.SemaphoreType.DMA],
        compiler_params=PARAMS,
        cost_estimate=pl.CostEstimate(flops=flops, bytes_accessed=0, transcendentals=0),
    )(source, *ahead)


def add_products(pairs, offsets, out_cols, left, entries, total, paired):
    ncol = len(left)
    outs = out_cols.shape[1] // ncol
    block = left[0][0].shape[1]
    rows = out_cols.shape[0]
    slots_dev = out_cols.shape[1] // ncol
    cap = rows * slots_dev
    shards, indices = [], [pairs, out_cols.astype(jnp.float32)]

    def number(array, known):
        for n, x in enumerate(known):
            if x is array:
                return n
        known.append(array)
        return len(known) - 1

    left_at = [[number(x, shards) for x in part] for part in left]
    plan = [
        (offsets.index(d), p, number(cols, indices), start, [(number(x, shards), half) for x, half in pieces], lefts)
        for d, p, (cols, start), pieces, lefts in entries
    ]
    has_total = total is not None

    def kernel(*refs):
        index_refs, refs = refs[:len(indices)], refs[len(indices):]
        sums = refs[-1]
        sums[...] = refs[-2][...] if has_total else jnp.zeros_like(sums)
        col_at = lax.axis_index("col")

        def tile(n, at):
            return refs[n][pl.ds(pl.multiple_of(at * block, block), block), :]

        def run(p):
            for n, q, source, start, pieces, lefts in plan:
                if q is not None and q != p:
                    continue
                for half in lefts:
                    head = half * len(offsets) + n
                    left_shard = left_at[half][p if len(left_at[half]) > 1 else 0]

                    def one_pair(m, carry):
                        pair = index_refs[0][head, m]
                        here, local = lax.div(pair, rows), lax.rem(pair, rows)
                        i = lax.div(here, slots_dev)
                        wanted = [index_refs[1][i, col_at * outs + o] for o in range(outs)]
                        found = []
                        for shard, piece_half in pieces:
                            for t in range(slots_dev):
                                column = index_refs[source][local, start + lax.rem(col_at + piece_half, ncol) * slots_dev + t]
                                found += [(column == wanted[o], shard, t, o) for o in range(outs)]

                        @pl.when(functools.reduce(jnp.logical_or, [match for match, *_ in found]))
                        def _():
                            for match, shard, t, o in found:

                                @pl.when(match)
                                def _():
                                    sums[i, o] += product(tile(left_shard, here), tile(shard, local * slots_dev + t))

                        return carry

                    lax.fori_loop(0, index_refs[0][head, cap], one_pair, 0)

        by_parity(paired, run)

    operands = shards + ([total] if has_total else [])
    shape = (rows, outs, block, block)
    return pl.pallas_call(
        kernel,
        out_shape=jax.ShapeDtypeStruct(shape, jnp.float32),
        in_specs=[SMEM] * len(indices) + [VMEM] * len(operands),
        out_specs=VMEM,
        compiler_params=PARAMS,
        cost_estimate=SOON,
    )(*indices, *operands)


def finish(pairs, offsets, tables, wanted_at, left, rights, entries, total):
    rows, outs, block = total.shape[:3]
    nright = max(len(part) for part in rights)
    slots_dev = outs
    ncol = left.shape[0] // (rows * slots_dev * block)
    blocks = rows * slots_dev
    tall = blocks * block
    cap = blocks
    targets = rows * outs
    longest = ncol * blocks * outs * slots_dev * max(sum(len(pieces) for *_, pieces in part) for part in entries)
    shards, indices = [left], [pairs, tables]

    def number(array, known):
        for n, x in enumerate(known):
            if x is array:
                return n
        known.append(array)
        return len(known) - 1

    rights_at = [[number(x, shards) for x in part] for part in rights]
    plan = [[(offsets.index(d), start, pieces) for d, start, pieces in part] for part in entries]

    def kernel(*refs):
        brought, refs = refs[:len(indices)], refs[len(indices):]
        total_ref, out_ref, right, sums, listed, touched, sems, index_sems, out_sems = refs[len(shards):len(shards) + 9]
        index_refs = refs[len(shards) + 9:]
        index_copies = [pltpu.make_async_copy(x, y, index_sems.at[n]) for n, (x, y) in enumerate(zip(brought, index_refs))]
        for copy in index_copies:
            copy.start()
        lefts = refs[0]
        pairs_ref, tables_ref = index_refs
        col_at = lax.axis_index("col")

        def run(p):
            copies = [
                pltpu.make_async_copy(refs[n].at[pl.ds(0, tall)], right.at[pl.ds(m * tall, tall)], sems.at[m])
                for m, n in enumerate(rights_at[p])
            ]
            copies.append(pltpu.make_async_copy(total_ref, sums.at[pl.ds(0, targets)], sems.at[nright]))
            for copy in copies:
                copy.start()

            for copy in index_copies:
                copy.wait()
            long = jnp.int32(0)
            for n, start, pieces in plan[p]:
                for half in range(ncol):
                    head = half * len(offsets) + n

                    def one_pair(m, long):
                        pair = pairs_ref[head, m]
                        here, local = lax.div(pair, rows), lax.rem(pair, rows)
                        i = lax.div(here, slots_dev)
                        wanted = [tables_ref[i, wanted_at + col_at * outs + o] for o in range(outs)]
                        found = []
                        for shard, piece_half in pieces:
                            for t in range(slots_dev):
                                column = tables_ref[local, start + lax.rem(col_at + piece_half, ncol) * slots_dev + t]
                                found += [(column == wanted[o], shard * blocks + t, o) for o in range(outs)]

                        def append(long):
                            for match, offset, o in found:
                                tiles = (half * blocks + here) * nright * blocks + offset + local * slots_dev
                                listed[long] = tiles * targets + i * outs + o
                                long += match.astype(jnp.int32)
                            return long

                        some_match = functools.reduce(jnp.logical_or, [match for match, *_ in found])
                        return lax.cond(some_match, append, lambda long: long, long)

                    long = lax.fori_loop(0, pairs_ref[head, cap], one_pair, long)
            for copy in copies:
                copy.wait()

            def tile(ref, at):
                return ref[pl.ds(pl.multiple_of(at * block, block), block), :]

            def some(m, carry):
                found = []
                for n in range(TOGETHER):
                    at = m * TOGETHER + n
                    code = listed[jnp.minimum(at, long - 1)]
                    tiles, target = lax.div(code, targets), lax.rem(code, targets)
                    result = product(tile(lefts, lax.div(tiles, nright * blocks)), tile(right, lax.rem(tiles, nright * blocks)))
                    found.append((jnp.where(at < long, target, targets), result))
                for target, result in found:
                    sums[target] += result
                    touched[target] = 1
                return carry

            lax.fori_loop(0, lax.div(long + TOGETHER - 1, TOGETHER), some, 0)

        early = pltpu.make_async_copy(total_ref, out_ref, sems.at[nright + 1])
        early.start()
        for n in range(targets + 1):
            touched[n] = 0
        by_parity(True, run)
        early.wait()
        for run in ("start", "wait"):
            for n in range(targets):
                copy = pltpu.make_async_copy(sums.at[n], out_ref.at[n], out_sems.at[n])
                pl.when(touched[n] == 1)(getattr(copy, run))

    result = pl.pallas_call(
        kernel,
        out_shape=jax.ShapeDtypeStruct((targets, block, block), jnp.float32),
        in_specs=[VMEM] * (len(indices) + len(shards) + 1),
        out_specs=pl.BlockSpec(memory_space=pltpu.HBM),
        scratch_shapes=[
            pltpu.VMEM((nright * tall, block), jnp.float32),
            pltpu.VMEM((targets + 1, block, block), jnp.float32),
            pltpu.SMEM((longest + 1,), jnp.int32),
            pltpu.SMEM((targets + 1,), jnp.int32),
            pltpu.SemaphoreType.DMA((nright + 2,)),
            pltpu.SemaphoreType.DMA((len(indices),)),
            pltpu.SemaphoreType.DMA((targets,)),
        ]
        + [pltpu.SMEM(x.shape, x.dtype) for x in indices],
        compiler_params=PARAMS,
        cost_estimate=SOON,
    )(*indices, *shards, total.reshape(targets, block, block))
    return result.reshape(total.shape)


def on_device(p_vals, p_cols, out_cols):
    nrow, ncol = lax.axis_size("row"), lax.axis_size("col")
    rows = p_cols.shape[0]

    def permute(x, source):
        pairs = []
        for r in range(nrow):
            for c in range(ncol):
                if source(r, c) is not None:
                    from_row, from_col = source(r, c)
                    pairs.append((from_row % nrow * ncol + from_col % ncol, r * ncol + c))
        return lax.ppermute(x, ("row", "col"), pairs)

    def after(x, *others):
        return lax.optimization_barrier((x, *others))[0]

    own = p_vals.reshape(-1, p_vals.shape[-1])
    offsets = tuple(range(1 - WINDOW, ncol))
    pairs = list_pairs(p_cols, ncol, offsets)

    if ncol == 2 and nrow % 2 == 0 and rows <= SUBLANES and 9 * p_cols.shape[1] <= own.shape[1]:
        def by_core(from_even, from_odd):
            return lambda r, c: (from_odd if r % 2 else from_even)(r, c)

        def across(r, c):
            return r, c + 1

        def behind(r, c):
            return r - 2, c

        def ahead(r, c):
            return r + 2, c

        def beside(r, c):
            return r ^ 1, c

        both = (0, 1)
        tall = own.shape[0]
        first = permute(own, by_core(across, behind))
        own_cols = p_cols.astype(jnp.float32)
        mate_cols = permute(own_cols, beside)
        beside_own = permute(own, beside)
        packed = pack(own, [own_cols, mate_cols, out_cols.astype(jnp.float32)], pairs)
        second = permute(packed, by_core(behind, across))
        next_first = permute(first, lambda r, c: (r + 1, c))
        third = permute(first, lambda r, c: (r, c + 1) if r % 2 else None)
        outgoing = repack(tall, (second, second), (beside_own, packed))
        fourth = permute(outgoing, by_core(across, ahead))
        left = [[packed], [first, second]]

        beside_other = permute(repack(tall, (first, second), (second, second)), beside)
        back_cols = index_tile(second, tall, 0, outgoing)
        width = 3 * p_cols.shape[1]
        own_at, mate_at, wanted_at = (n * p_cols.shape[1] for n in range(3))

        def add(entries, total):
            return add_products(pairs, offsets, out_cols, left, entries, total, True)

        total = add(
            [
                (0, 0, (own_cols, 0), [(packed, 0), (first, 1)], both),
                (0, 1, (own_cols, 0), [(packed, 0), (second, 1)], both),
                (1, 0, (mate_cols, 0), [(beside_own, 0)], both),
                (-1, 1, (mate_cols, 0), [(beside_own, 0)], both),
                (-2, 0, (back_cols, own_at), [(second, 0)], both),
            ],
            None,
        )
        passed_on = repack(tall, (third, packed), (third, packed), total)
        beside_third = permute(passed_on, lambda r, c: None if r % 2 else (r + 1, c))
        mate_back_cols = index_tile(beside_other, tall, 0)
        total = add(
            [
                (1, 0, (mate_cols, 0), [(beside_other, 1)], both),
                (-1, 1, (mate_cols, 0), [(beside_other, 1)], both),
                (-2, 1, (mate_back_cols, mate_at), [(first, 0), (third, 1)], both),
                (-1, 0, (back_cols, mate_at), [(next_first, 0)], both),
            ],
            total,
        )
        late_cols = index_tile(second, tall, 10**9, next_first)
        far_cols = index_tile(fourth, tall, 10**9, late_cols, total)
        tables = beside_each_other(rows, width, (packed, packed), (late_cols, beside_other), (far_cols, far_cols))
        return finish(
            pairs,
            offsets,
            tables,
            wanted_at,
            stack(tall, (packed, first), (packed, second)),
            [[fourth, beside_third], [fourth, next_first]],
            [
                [
                    (-2, width + own_at, [(0, 1)]),
                    (-1, width + mate_at, [(1, 1)]),
                ],
                [
                    (1, 2 * width + mate_at, [(0, 0), (1, 1)]),
                ],
            ],
            total,
        )

    left = [[own]] + [[permute(own, lambda r, c, j=j: (r, c + j))] for j in range(1, ncol)]
    halves = tuple(range(ncol))
    own_cols = p_cols.astype(jnp.float32)
    shards, cols = {0: own}, {0: own_cols}
    for d in offsets:
        if d:
            shards[d], cols[d] = (permute(x, lambda r, c, d=d: (r + d, c)) for x in (own, own_cols))
    total = None
    for j in halves:
        sources = {d: after(x, total) if j else x for d, x in shards.items()}
        layer = {d: permute(x, lambda r, c, j=j: (r, c + j)) if j else x for d, x in sources.items()}
        entries = [(d, None, (cols[d], 0), [(x, j)], halves) for d, x in layer.items()]
        total = add_products(pairs, offsets, out_cols, left, entries, total, False)
    return total


def solution(mesh):
    placed = (P("row", "col", None, None), P("row", None), P("row", None))
    return jax.shard_map(
        on_device,
        mesh=mesh,
        in_specs=placed,
        out_specs=P("row", "col", None, None),
        check_vma=False,
    )
```
